32 devices in a mesh: shards: 4 (over z), context: 2 (over y), tensor: 4 (over x, core).
Axes of the slice: x: 2, y: 2, z: 4, core: 2. Of those that a mesh axis runs over, the one named last changes fastest.
Arguments:
- tokens: bfloat16 [8, 2048, 768], P('shards', 'context'), may hold values from -6 to 6
- norm_gain: bfloat16 [768], replicated, may hold values from 0.099609375 to 1.8984375
- w_z: bfloat16 [768, 1536], P('shards', 'tensor'), may hold values from -0.21875 to 0.21875
- w_x: bfloat16 [768, 1536], P('shards', 'tensor'), may hold values from -0.21875 to 0.21875
- w_bc: bfloat16 [768, 256], P('shards'), may hold values from -0.21875 to 0.21875
- w_dt: bfloat16 [768, 24], P('shards', 'tensor'), may hold values from -0.21875 to 0.21875
- conv_x: bfloat16 [4, 1536], P(None, 'tensor'), may hold values from -3 to 3
- conv_bc: bfloat16 [4, 256], replicated, may hold values from -3 to 3
- dt_bias: float32 [24], P('tensor'), may hold values from -3 to -0.5
- a_log: float32 [24], P('tensor'), may hold values from -10 to -3
- skip: float32 [24], P('tensor'), may hold values from 0.5 to 1.5
- gate_gain: bfloat16 [1536], P('tensor'), may hold values from 0.099609375 to 1.8984375
- w_out: bfloat16 [1536, 768], P('tensor', 'shards'), may hold values from -0.15625 to 0.15625
- cotangent: bfloat16 [8, 2048, 768], P('shards', 'context'), may hold values from -6 to 6
Outputs:
- mixed: bfloat16 [8, 2048, 768], P('shards', 'context')
- grad_tokens: float32 [8, 2048, 768], P('shards', 'context')
- grad_norm_gain: float32 [768], replicated
- grad_w_z: float32 [768, 1536], P(('shards', 'context'), 'tensor')
- grad_w_x: float32 [768, 1536], P(('shards', 'context'), 'tensor')
- grad_w_bc: float32 [768, 256], P(('shards', 'context'))
- grad_w_dt: float32 [768, 24], P(('shards', 'context'), 'tensor')
- grad_conv_x: float32 [4, 1536], P(None, 'tensor')
- grad_conv_bc: float32 [4, 256], replicated
- grad_dt_bias: float32 [24], P('tensor')
- grad_a_log: float32 [24], P('tensor')
- grad_skip: float32 [24], P('tensor')
- grad_gate_gain: float32 [1536], P('tensor')
- grad_w_out: float32 [1536, 768], P('tensor', ('shards', 'context'))
The draws below stay inside these ranges and needn't reach their ends.
All inputs are finite; a program needn't handle non-finite values.
Results may differ from the reference program's by a relative error of at most 0.012.
The reference program's roundings to bfloat16 on the way count: a program that leaves them out, or rounds other values in their place, can miss the bound.
Values may be sent and summed in bfloat16 or wider, within the bound.
A program may use at most 192 MiB of HBM per device.

```python
import jax
import jax.numpy as jnp
from jax import lax

D = 768
HEADS = 24
HEAD_DIM = 64
STATE = 128
WIDTH = 4
BLOCK = 256
SEQ_LEN = 2048
INNER = 1536
SEQS = 8


def draw_a_log(key, part):
    key = jax.random.fold_in(key, 7)
    return jax.random.uniform(key, (HEADS,), jnp.float32, -9.0, -3.0)


def block_scale(own_key, dims, cuts, least, high):
    def one(axis_at, parts):
        draws = jax.random.uniform(jax.random.fold_in(jax.random.fold_in(own_key, 6), axis_at), (parts,), jnp.float32, least / len(cuts), high / len(cuts))
        return jnp.repeat(jnp.exp(draws), dims[axis_at] // parts).reshape((-1,) + (1,) * (len(dims) - axis_at - 1))

    loudness = one(*cuts[0])
    for cut in cuts[1:]:
        loudness = loudness * one(*cut)
    return loudness


def noise(stream_key, shape, scale, bound, cuts=(), kind=jnp.bfloat16):
    factor_of = block_scale(stream_key, shape, cuts, -0.22, 0.18) if cuts else 1.0
    entries = jax.random.normal(stream_key, shape, jnp.float32) * scale * factor_of
    return jnp.minimum(jnp.maximum(entries, -bound), bound).astype(kind)


def setup_inputs(seed: int = 0) -> dict:
    key_list = jax.random.split(jax.random.key(seed), 15)
    tokens = noise(key_list[0], (SEQS, SEQ_LEN, D), 1.0, 6.0, ((0, 4), (1, 2)))
    norm_gain = jnp.clip(1.0 + 0.18 * jax.random.normal(key_list[1], (D,), jnp.float32), 0.099609375, 1.8984375).astype(jnp.bfloat16)
    w_z = noise(key_list[2], (D, INNER), D ** -0.5, 0.21875, ((0, 4), (1, 4)))
    w_x = noise(key_list[3], (D, INNER), D ** -0.5, 0.21875, ((0, 4), (1, 4)))
    w_bc = noise(key_list[4], (D, 2 * STATE), D ** -0.5, 0.21875, ((0, 4),))
    w_dt = noise(key_list[5], (D, HEADS), D ** -0.5, 0.21875, ((0, 4), (1, 4)))
    conv_x = noise(key_list[6], (WIDTH, INNER), WIDTH ** -0.5, 3.0, ((1, 4),))
    conv_bc = noise(key_list[7], (WIDTH, 2 * STATE), WIDTH ** -0.5, 3.0)
    dt_bias = jnp.clip(-3.0 + 2.5 * jax.random.uniform(key_list[8], (HEADS,), jnp.float32) ** block_scale(key_list[8], (HEADS,), ((0, 4),), -0.2, 0.2), -3.0, -0.5)
    a_log = draw_a_log(jax.random.fold_in(key_list[14], 71), 0)
    skip = jnp.clip(0.5 + 1.0 * jax.random.uniform(key_list[10], (HEADS,), jnp.float32) ** block_scale(key_list[10], (HEADS,), ((0, 4),), -0.2, 0.2), 0.5, 1.5)
    gate_gain = jnp.clip(1.0 + 0.18 * jax.random.normal(key_list[11], (INNER,), jnp.float32), 0.099609375, 1.8984375).astype(jnp.bfloat16)
    w_out = noise(key_list[12], (INNER, D), INNER ** -0.5, 0.15625, ((0, 4), (1, 4)))
    cotangent = noise(key_list[13], (SEQS, SEQ_LEN, D), 1.0, 6.0, ((0, 4), (1, 2)))
    return {"tokens": tokens, "norm_gain": norm_gain, "w_z": w_z, "w_x": w_x, "w_bc": w_bc, "w_dt": w_dt, "conv_x": conv_x, "conv_bc": conv_bc, "dt_bias": dt_bias, "a_log": a_log, "skip": skip, "gate_gain": gate_gain, "w_out": w_out, "cotangent": cotangent}


epsilon = 1e-05
highest = lax.Precision.HIGHEST

@jax.custom_vjp
def low(v):
    return lax.optimization_barrier(v.astype(jnp.bfloat16)).astype(jnp.float32)

@jax.custom_vjp
def low_back(v):
    return v

def low_keep(v):
    return (low(v), None)

def low_pass(kept, grad):
    return (grad,)

def back_keep(v):
    return (v, None)

def back_low(kept, grad):
    return (low(grad),)
low.defvjp(low_keep, low_pass)
low_back.defvjp(back_keep, back_low)

def matmul(left, right):
    return jnp.dot(left, right, precision=highest, preferred_element_type=jnp.float32)

def causal_conv(signal, weights):
    padded = jnp.concatenate([jnp.zeros((WIDTH - 1, signal.shape[1]), jnp.float32), signal], axis=0)
    total = weights[0] * padded[0:SEQ_LEN]
    for offset in range(1, WIDTH):
        total = total + weights[offset] * padded[offset:offset + SEQ_LEN]
    return total

def block_step(state, pieces, rate, skip):
    x_block, b_block, c_block, step_block = pieces
    decay_sum = jnp.cumsum(step_block * rate, axis=0)
    last_sum = decay_sum[-1]
    causal = lax.broadcasted_iota(jnp.int32, (BLOCK, BLOCK), 0) >= lax.broadcasted_iota(jnp.int32, (BLOCK, BLOCK), 1)
    gram_matrix = matmul(c_block, b_block.T)
    spacing = decay_sum[:, None, :] - decay_sum[None, :, :]
    within = jnp.where(causal[:, :, None], jnp.exp(jnp.where(causal[:, :, None], spacing, 0.0)), 0.0)
    mixing = low(gram_matrix[:, :, None] * within * step_block[None, :, :])
    intra = jnp.einsum('ijh,jhp->ihp', mixing, x_block, precision=highest)
    reached = jnp.einsum('in,hnp->ihp', c_block, state, precision=highest)
    scanned = intra + jnp.exp(decay_sum)[:, :, None] * reached + skip[None, :, None] * x_block
    toward = jnp.exp(last_sum[None, :] - decay_sum) * step_block
    loaded = low(b_block[:, None, :] * toward[:, :, None])
    fresh_state = jnp.einsum('jhn,jhp->hnp', loaded, x_block, precision=highest)
    return (jnp.exp(last_sum)[:, None, None] * state + fresh_state, scanned)

def sequence_forward(params, sequence):
    norm_gain, w_z, w_x, w_bc, w_dt, conv_x, conv_bc, dt_bias, a_log, skip, gate_gain, w_out = params
    row_scale = lax.rsqrt(lax.optimization_barrier(jnp.mean(sequence * sequence, axis=-1, keepdims=True)) + epsilon)
    normed = low(sequence * row_scale * norm_gain)
    gate_value = low_back(matmul(normed, w_z))
    x_pre = low_back(low(matmul(normed, w_x)))
    bc_pre = low_back(low(matmul(normed, w_bc)))
    dt_raw = low_back(matmul(normed, w_dt))
    x_act = low(jax.nn.silu(causal_conv(x_pre, conv_x)))
    bc_act = low(jax.nn.silu(causal_conv(bc_pre, conv_bc)))
    step_size = jax.nn.softplus(dt_raw + dt_bias)
    rate = -jnp.exp(a_log)
    block_count = SEQ_LEN // BLOCK
    pieces = (x_act.reshape(block_count, BLOCK, HEADS, HEAD_DIM), bc_act[:, :STATE].reshape(block_count, BLOCK, STATE), bc_act[:, STATE:].reshape(block_count, BLOCK, STATE), step_size.reshape(block_count, BLOCK, HEADS))

    def advance(state, piece):
        return block_step(state, piece, rate, skip)
    start_state = jnp.zeros((HEADS, STATE, HEAD_DIM), jnp.float32)
    scanned = lax.scan(jax.checkpoint(advance), start_state, pieces)[1]
    scanned = low_back(scanned.reshape(SEQ_LEN, INNER))
    gated_out = scanned * jax.nn.silu(gate_value)
    spread = lax.optimization_barrier(jnp.mean(gated_out * gated_out, axis=-1, keepdims=True))
    projected = low_back(matmul(low(gated_out * gate_gain), w_out))
    return sequence + projected * lax.rsqrt(spread + epsilon)

def reference(tokens, norm_gain, w_z, w_x, w_bc, w_dt, conv_x, conv_bc, dt_bias, a_log, skip, gate_gain, w_out, cotangent):
    params = (norm_gain.astype(jnp.float32), w_z.astype(jnp.float32), w_x.astype(jnp.float32), w_bc.astype(jnp.float32), w_dt.astype(jnp.float32), conv_x.astype(jnp.float32), conv_bc.astype(jnp.float32), dt_bias.astype(jnp.float32), a_log.astype(jnp.float32), skip.astype(jnp.float32), gate_gain.astype(jnp.float32), w_out.astype(jnp.float32))
    inputs = tokens.astype(jnp.float32)

    def forward(weights, sequences):

        def one(carried, sequence):
            return (carried, sequence_forward(weights, sequence))
        return lax.scan(one, jnp.zeros((), jnp.float32), sequences)[1]
    mixed, pullback = jax.vjp(forward, params, inputs)
    grad_params, grad_tokens = pullback(cotangent.astype(jnp.float32))
    return (mixed.astype(jnp.bfloat16), grad_tokens, grad_params[0], grad_params[1], grad_params[2], grad_params[3], grad_params[4], grad_params[5], grad_params[6], grad_params[7], grad_params[8], grad_params[9], grad_params[10], grad_params[11])
```

```python
import jax
import jax.numpy as jnp
from jax import lax
from jax.sharding import PartitionSpec as P

BLOCK = 256
INNER = 1536


epsilon = 1e-05
highest = lax.Precision.HIGHEST


def from_behind(value, axis, steps):
    count = lax.axis_size(axis)
    first, last = (max(0, -steps), min(count, count - steps))
    return lax.ppermute(value, axis, [(source, source + steps) for source in range(first, last)])


def product(left, right):
    return jnp.dot(left, right, preferred_element_type=jnp.float32)


def product_transposed(left, right):
    return lax.dot_general(
        left, right, (((1,), (1,)), ((), ())), preferred_element_type=jnp.float32
    )


def product_over_rows(left, right):
    return lax.dot_general(
        left, right, (((0,), (0,)), ((), ())), preferred_element_type=jnp.float32
    )


def depthwise(signal, edge_rows, weights):
    tap_count = weights.shape[0]
    span_len = signal.shape[1]
    padded = jnp.concatenate([edge_rows, signal], axis=1).astype(jnp.float32)
    wide_taps = weights.astype(jnp.float32)
    total = wide_taps[0] * padded[:, 0:span_len]
    for offset in range(1, tap_count):
        total = total + wide_taps[offset] * padded[:, offset : offset + span_len]
    return (total, padded)


def depthwise_back(grad_conv, edge_rows, weights, padded):
    tap_count = weights.shape[0]
    span_len = grad_conv.shape[1]
    wide_taps = weights.astype(jnp.float32)
    extended = jnp.concatenate([grad_conv, edge_rows], axis=1)
    grad_signal = wide_taps[tap_count - 1] * extended[:, 0:span_len]
    for offset in range(1, tap_count):
        grad_signal = (
            grad_signal
            + wide_taps[tap_count - 1 - offset] * extended[:, offset : offset + span_len]
        )
    grad_taps = jnp.stack(
        [
            jnp.sum(grad_conv * padded[:, offset : offset + span_len], axis=(0, 1))
            for offset in range(tap_count)
        ]
    )
    return (grad_signal, grad_taps)


def silu_slope(value):
    sigma = jax.nn.sigmoid(value)
    return sigma * (1.0 + value * (1.0 - sigma))


def on_device(
    tokens,
    norm_gain,
    w_z,
    w_x,
    w_bc,
    w_dt,
    conv_x,
    conv_bc,
    dt_bias,
    a_log,
    skip,
    gate_gain,
    w_out,
    cotangent,
):
    seq_count, span_len, model_width = tokens.shape
    row_count = seq_count * span_len
    head_count = dt_bias.shape[0]
    state_size = w_bc.shape[1] // 2
    tap_count = conv_x.shape[0]
    block_count = span_len // BLOCK
    inner_part = w_z.shape[1]
    packed = jnp.concatenate(
        [w_x, w_bc, jnp.pad(w_dt, ((0, 0), (0, 128 - head_count))), w_z, w_out.T], axis=1
    )
    full = lax.all_gather(packed, "shards", axis=0, tiled=True)
    at_z = inner_part + 2 * state_size + 128
    full_x = full[:, :inner_part]
    full_bc = full[:, inner_part : inner_part + 2 * state_size]
    full_dt = full[:, inner_part + 2 * state_size : inner_part + 2 * state_size + head_count]
    full_z = full[:, at_z : at_z + inner_part]
    out_t = full[:, at_z + inner_part :]
    inner_width = full_z.shape[1]
    head_width = inner_width // head_count
    flat_rows = tokens.reshape(row_count, model_width).astype(jnp.float32)
    row_scale = lax.rsqrt(jnp.mean(flat_rows * flat_rows, axis=1, keepdims=True) + epsilon)
    unit_rows = flat_rows * row_scale
    gain_input = norm_gain.astype(jnp.float32)
    normed = (unit_rows * gain_input).astype(jnp.bfloat16)
    fronts = product(normed, full[:, : at_z + inner_part])
    gate_value = fronts[:, at_z:]
    pre = fronts[:, : inner_part + 2 * state_size].astype(jnp.bfloat16)
    pre = pre.reshape(seq_count, span_len, inner_part + 2 * state_size)
    x_pre, bc_pre = pre[..., :inner_part], pre[..., inner_part:]
    dt_raw = fronts[:, inner_part + 2 * state_size : inner_part + 2 * state_size + head_count]
    edge = from_behind(pre[:, span_len - tap_count + 1 :], "context", 1)
    x_edge, bc_edge = edge[..., :inner_part], edge[..., inner_part:]
    x_conv, x_padded = depthwise(x_pre, x_edge, conv_x)
    bc_conv, bc_padded = depthwise(bc_pre, bc_edge, conv_bc)
    x_act = jax.nn.silu(x_conv).astype(jnp.bfloat16)
    bc_act = jax.nn.silu(bc_conv).astype(jnp.bfloat16)
    x_blocks = x_act.reshape(seq_count, block_count, BLOCK, head_count, head_width)
    b_in = bc_act[:, :, :state_size].reshape(seq_count, block_count, BLOCK, state_size)
    c_in = bc_act[:, :, state_size:].reshape(seq_count, block_count, BLOCK, state_size)
    pre_step = dt_raw + dt_bias
    step_size = jax.nn.softplus(pre_step)
    rate = -jnp.exp(a_log)
    step_heads = jnp.transpose(
        step_size.reshape(seq_count, block_count, BLOCK, head_count), (0, 1, 3, 2)
    )
    lower = jnp.tril(jnp.ones((BLOCK, BLOCK), jnp.float32))
    decay_sum = jnp.einsum("schj,ij->schi", step_heads * rate[:, None], lower, precision=highest)
    last_sum = decay_sum[..., -1]
    causal = lax.broadcasted_iota(jnp.int32, (BLOCK, BLOCK), 0) >= lax.broadcasted_iota(
        jnp.int32, (BLOCK, BLOCK), 1
    )
    gram_matrix = jnp.einsum("scin,scjn->scij", c_in, b_in, preferred_element_type=jnp.float32)
    spacing = decay_sum[..., :, None] - decay_sum[..., None, :]
    within = jnp.where(causal, jnp.exp(jnp.where(causal, spacing, 0.0)), 0.0)
    masked_within = within * step_heads[..., None, :]
    mix_full = gram_matrix[:, :, None] * masked_within
    mixing = mix_full.astype(jnp.bfloat16)
    intra = jnp.einsum("schij,scjhp->scihp", mixing, x_blocks, preferred_element_type=jnp.float32)
    toward = jnp.exp(last_sum[..., None] - decay_sum) * step_heads
    b_wide = b_in.astype(jnp.float32)
    loaded = (b_wide[:, :, None] * toward[..., None]).astype(jnp.bfloat16)
    fresh_state = jnp.einsum(
        "schjn,scjhp->schnp", loaded, x_blocks, preferred_element_type=jnp.float32
    )
    carried = jnp.zeros((seq_count, head_count, state_size, head_width), jnp.float32)
    entering = []
    for index in range(block_count):
        entering.append(carried)
        carried = jnp.exp(last_sum[:, index])[:, :, None, None] * carried + fresh_state[:, index]
    device_total = jnp.sum(last_sum, axis=1)
    device_decay = jnp.exp(device_total)
    incoming = from_behind(carried, "context", 1)
    after_sum = jnp.cumsum(last_sum, axis=1)
    start_decay = jnp.exp(after_sum - last_sum)
    enter_true = jnp.stack(entering, axis=1) + start_decay[..., None, None] * incoming[:, None]
    c_wide = c_in.astype(jnp.float32)
    reached = jnp.einsum("scin,schnp->scihp", c_wide, enter_true, precision=highest)
    growth = jnp.exp(jnp.transpose(decay_sum, (0, 1, 3, 2)))
    x_wide = x_blocks.astype(jnp.float32)
    scanned = intra + growth[..., None] * reached + skip[:, None] * x_wide
    scanned = scanned.reshape(row_count, inner_width)
    sigma_gate = jax.nn.sigmoid(gate_value)
    silu_gate = gate_value * sigma_gate
    gated_out = scanned * silu_gate
    gain_gate = gate_gain.astype(jnp.float32)
    weighted = (gated_out * gain_gate).astype(jnp.bfloat16)
    partial_value = product_transposed(weighted, out_t)
    square_sums = jnp.sum(gated_out * gated_out, axis=1)
    grad_rows = cotangent.reshape(row_count, model_width).astype(jnp.float32)
    scale_part = jnp.sum(grad_rows * partial_value, axis=1)
    squares, grad_scale = lax.psum(jnp.stack([square_sums, scale_part]), "tensor")
    own_rows = row_count // lax.axis_size("tensor")
    own_at = lax.axis_index("tensor") * own_rows

    def own(value):
        return lax.dynamic_slice_in_dim(value, own_at, own_rows, 0)

    out_scale = lax.rsqrt(squares / INNER + epsilon)
    own_projected = lax.psum_scatter(
        partial_value.astype(jnp.bfloat16), "tensor", scatter_dimension=0, tiled=True
    ).astype(jnp.float32)
    own_mixed = (own(flat_rows) + own_projected * own(out_scale)[:, None]).astype(jnp.bfloat16)
    mixed = lax.all_gather(own_mixed, "tensor", axis=0, tiled=True).reshape(tokens.shape)
    grad_spread = -0.5 * grad_scale * out_scale * out_scale * out_scale
    grad_proj = (grad_rows * out_scale[:, None]).astype(jnp.bfloat16)
    grad_weighted = product(grad_proj, out_t)
    grad_out_t = product_over_rows(grad_proj, weighted)
    final_out = lax.psum_scatter(
        grad_out_t.astype(jnp.bfloat16), ("shards", "context"), scatter_dimension=0, tiled=True
    ).astype(jnp.float32).T
    grad_gate_gain = jnp.sum(grad_weighted * gated_out, axis=0)
    grad_gated = grad_weighted * gain_gate + 2.0 / INNER * grad_spread[:, None] * gated_out
    grad_scanned = (grad_gated * silu_gate).astype(jnp.bfloat16)
    grad_gate = (
        grad_gated * scanned * sigma_gate * (1.0 + gate_value * (1.0 - sigma_gate))
    ).astype(jnp.bfloat16)
    final_z = lax.psum_scatter(
        product_over_rows(normed, grad_gate).astype(jnp.bfloat16),
        ("shards", "context"),
        scatter_dimension=0,
        tiled=True,
    ).astype(jnp.float32)
    grad_blocks = grad_scanned.reshape(seq_count, block_count, BLOCK, head_count, head_width)
    grad_wide = grad_blocks.astype(jnp.float32)
    grad_skip = jnp.sum(grad_wide * x_wide, axis=(0, 1, 2, 4))
    grad_reached = grad_wide * growth[..., None]
    from_output = jnp.einsum("scin,scihp->schnp", c_wide, grad_reached, precision=highest)
    carried_back = jnp.zeros_like(carried)
    leaving = []
    for index in range(block_count - 1, -1, -1):
        leaving.append(carried_back)
        carried_back = (
            from_output[:, index] + jnp.exp(last_sum[:, index])[:, :, None, None] * carried_back
        )
    outgoing = from_behind(carried_back, "context", -1)
    end_decay = jnp.exp(device_total[:, None] - after_sum)
    leave_true = jnp.stack(leaving[::-1], axis=1) + end_decay[..., None, None] * outgoing[:, None]
    grad_x_blocks = skip[:, None] * grad_wide
    grad_x_blocks = grad_x_blocks + jnp.einsum(
        "schij,scihp->scjhp", mixing, grad_blocks, preferred_element_type=jnp.float32
    )
    grad_x_blocks = grad_x_blocks + jnp.einsum(
        "schjn,schnp->scjhp", loaded.astype(jnp.float32), leave_true, precision=highest
    )
    grad_mix = jnp.einsum(
        "scihp,scjhp->schij", grad_blocks, x_blocks, preferred_element_type=jnp.float32
    )
    grad_gram = jnp.sum(grad_mix * masked_within, axis=2)
    grad_step = jnp.sum(grad_mix * gram_matrix[:, :, None] * within, axis=3)
    spread_term = grad_mix * mix_full
    grad_cum = jnp.sum(spread_term, axis=4) - jnp.sum(spread_term, axis=3)
    grad_c_in = jnp.einsum("scij,scjn->scin", grad_gram, b_wide, precision=highest)
    grad_c_in = grad_c_in + jnp.einsum(
        "scihp,schnp->scin", grad_reached, enter_true, precision=highest
    )
    grad_b_in = jnp.einsum("scij,scin->scjn", grad_gram, c_wide, precision=highest)
    grad_cum = grad_cum + jnp.transpose(jnp.sum(grad_reached * reached, axis=4), (0, 1, 3, 2))
    grad_last = jnp.sum(leave_true * enter_true, axis=(3, 4)) * jnp.exp(last_sum)
    grad_loaded = jnp.einsum("scjhp,schnp->schjn", x_wide, leave_true, precision=highest)
    grad_b_in = grad_b_in + jnp.sum(grad_loaded * toward[..., None], axis=2)
    touch = jnp.sum(grad_loaded * b_wide[:, :, None], axis=4)
    touch_part = touch * toward
    grad_step = grad_step + touch * jnp.exp(last_sum[..., None] - decay_sum)
    grad_last = grad_last + jnp.sum(touch_part, axis=3)
    grad_cum = (grad_cum - touch_part).at[..., -1].add(grad_last)
    grad_log = jnp.einsum("schi,ij->schj", grad_cum, lower, precision=highest)
    grad_step = grad_step + grad_log * rate[:, None]
    grad_a_log = jnp.sum(grad_log * step_heads, axis=(0, 1, 3)) * rate
    grad_pre = jnp.transpose(grad_step, (0, 1, 3, 2)).reshape(
        row_count, head_count
    ) * jax.nn.sigmoid(pre_step)
    grad_dt_bias = jnp.sum(grad_pre, axis=0)
    grad_dt_raw = grad_pre.astype(jnp.bfloat16)
    grad_x_conv = grad_x_blocks.reshape(seq_count, span_len, inner_width) * silu_slope(x_conv)
    grad_bc_act = jnp.concatenate([grad_b_in, grad_c_in], axis=3).reshape(
        seq_count, span_len, 2 * state_size
    )
    grad_bc_conv = grad_bc_act * silu_slope(bc_conv)
    following = from_behind(
        jnp.concatenate(
            [grad_x_conv[:, : tap_count - 1], grad_bc_conv[:, : tap_count - 1]], axis=2
        ),
        "context",
        -1,
    )
    x_next, bc_next = following[..., :inner_width], following[..., inner_width:]
    grad_x_signal, grad_conv_x = depthwise_back(grad_x_conv, x_next, conv_x, x_padded)
    grad_bc_signal, conv_bc_part = depthwise_back(grad_bc_conv, bc_next, conv_bc, bc_padded)
    grad_x_pre = grad_x_signal.reshape(row_count, inner_width).astype(jnp.bfloat16)
    normed_part = (
        product_transposed(grad_gate, full_z)
        + product_transposed(grad_x_pre, full_x)
        + product_transposed(grad_dt_raw, full_dt)
    )
    own_bc = lax.psum_scatter(
        grad_bc_signal.reshape(row_count, 2 * state_size),
        "tensor",
        scatter_dimension=0,
        tiled=True,
    ).astype(jnp.bfloat16)
    own_grad = lax.psum_scatter(
        normed_part.astype(jnp.bfloat16), "tensor", scatter_dimension=0, tiled=True
    ).astype(jnp.float32)
    own_grad = own_grad + product_transposed(own_bc, full_bc)
    own_unit = own(unit_rows)
    grad_norm_gain = jnp.sum(own_grad * own_unit, axis=0)
    grad_unit = own_grad * gain_input
    own_tokens = own(grad_rows) + own(row_scale) * (
        grad_unit - own_unit * jnp.mean(grad_unit * own_unit, axis=1, keepdims=True)
    )
    grad_tokens = lax.all_gather(
        own_tokens.astype(jnp.bfloat16), "tensor", axis=0, tiled=True
    ).astype(jnp.float32)
    back = jnp.concatenate([grad_x_pre, grad_dt_raw], axis=1)
    grad_back = product_over_rows(normed, back)
    grad_w_bc = product_over_rows(own(normed), own_bc)
    final_back = lax.psum_scatter(
        jnp.concatenate([grad_back, grad_w_bc], axis=1).astype(jnp.bfloat16),
        ("shards", "context"),
        scatter_dimension=0,
        tiled=True,
    ).astype(jnp.float32)
    final_x = final_back[:, :inner_width]
    final_dt = final_back[:, inner_width : inner_width + head_count]
    whole = jnp.concatenate([grad_norm_gain, conv_bc_part.reshape(-1)])
    by_tensor = jnp.concatenate(
        [grad_conv_x.reshape(-1), grad_gate_gain, grad_dt_bias, grad_a_log, grad_skip]
    )
    final_bc = lax.psum(final_back[:, inner_width + head_count :], "tensor")
    places = lax.axis_size("tensor")
    here = lax.axis_index("tensor")
    spread_out = jnp.zeros((places, by_tensor.shape[0]), jnp.float32).at[here].set(by_tensor)
    sums = lax.psum(
        jnp.concatenate([whole, spread_out.reshape(-1)]), ("shards", "context", "tensor")
    )
    norm_sum = sums[:model_width]
    conv_bc_sum = sums[model_width : whole.shape[0]].reshape(conv_bc.shape)
    mine = lax.dynamic_index_in_dim(
        sums[whole.shape[0] :].reshape(places, -1), here, 0, keepdims=False
    )
    at = tap_count * inner_width
    conv_x_sum = mine[:at].reshape(tap_count, inner_width)
    gate_gain_sum = mine[at : at + inner_width]
    heads_sum = mine[at + inner_width :].reshape(3, head_count)
    return (
        mixed,
        grad_tokens.reshape(seq_count, span_len, model_width),
        norm_sum,
        final_z,
        final_x,
        final_bc,
        final_dt,
        conv_x_sum,
        conv_bc_sum,
        heads_sum[0],
        heads_sum[1],
        heads_sum[2],
        gate_gain_sum,
        final_out,
    )


def solution(mesh):
    placed = (
        P("shards", "context", None),
        P(),
        P("shards", "tensor"),
        P("shards", "tensor"),
        P("shards", None),
        P("shards", "tensor"),
        P(None, "tensor"),
        P(),
        P("tensor"),
        P("tensor"),
        P("tensor"),
        P("tensor"),
        P("tensor", "shards"),
        P("shards", "context", None),
    )
    return jax.shard_map(
        on_device,
        mesh=mesh,
        in_specs=placed,
        out_specs=(
            P("shards", "context", None),
            P("shards", "context", None),
            P(),
            P(("shards", "context"), "tensor"),
            P(("shards", "context"), "tensor"),
            P(("shards", "context"), None),
            P(("shards", "context"), "tensor"),
            P(None, "tensor"),
            P(),
            P("tensor"),
            P("tensor"),
            P("tensor"),
            P("tensor"),
            P("tensor", ("shards", "context")),
        ),
        check_vma=False,
    )
```

```python
import jax
import jax.numpy as jnp
from jax import lax
from jax.experimental import pallas as pl
from jax.experimental.pallas import tpu as pltpu
from jax.sharding import PartitionSpec as P

BLOCK = 256
INNER = 1536


epsilon = 1e-05
highest = lax.Precision.HIGHEST


def from_behind(value, axis, steps):
    count = lax.axis_size(axis)
    first, last = (max(0, -steps), min(count, count - steps))
    return lax.ppermute(value, axis, [(source, source + steps) for source in range(first, last)])


def product(left, right):
    return jnp.dot(left, right, preferred_element_type=jnp.float32)


def product_transposed(left, right):
    return lax.dot_general(
        left, right, (((1,), (1,)), ((), ())), preferred_element_type=jnp.float32
    )


def product_over_rows(left, right):
    return lax.dot_general(
        left, right, (((0,), (0,)), ((), ())), preferred_element_type=jnp.float32
    )


def depthwise(signal, edge_rows, weights):
    tap_count = weights.shape[0]
    span_len = signal.shape[1]
    padded = jnp.concatenate([edge_rows, signal], axis=1).astype(jnp.float32)
    wide_taps = weights.astype(jnp.float32)
    total = wide_taps[0] * padded[:, 0:span_len]
    for offset in range(1, tap_count):
        total = total + wide_taps[offset] * padded[:, offset : offset + span_len]
    return (total, padded)


def depthwise_back(grad_conv, edge_rows, weights, padded):
    tap_count = weights.shape[0]
    span_len = grad_conv.shape[1]
    wide_taps = weights.astype(jnp.float32)
    extended = jnp.concatenate([grad_conv, edge_rows], axis=1)
    grad_signal = wide_taps[tap_count - 1] * extended[:, 0:span_len]
    for offset in range(1, tap_count):
        grad_signal = (
            grad_signal
            + wide_taps[tap_count - 1 - offset] * extended[:, offset : offset + span_len]
        )
    grad_taps = jnp.stack(
        [
            jnp.sum(grad_conv * padded[:, offset : offset + span_len], axis=(0, 1))
            for offset in range(tap_count)
        ]
    )
    return (grad_signal, grad_taps)


def silu_slope(value):
    sigma = jax.nn.sigmoid(value)
    return sigma * (1.0 + value * (1.0 - sigma))


MESH = pl.DeviceIdType.MESH
IN_VMEM = pl.BlockSpec(memory_space=pltpu.VMEM)


def group_place():
    places = lax.axis_size("context")
    count = lax.axis_size("shards") * places
    mine = lax.axis_index("shards") * places + lax.axis_index("context")
    return count, mine


def group_peer(steps):
    count, mine = group_place()
    peer = lax.rem(mine + steps, count)
    places = lax.axis_size("context")
    return peer, {"shards": peer // places, "context": lax.rem(peer, places)}


def meet(devices):
    barrier = pltpu.get_barrier_semaphore()
    for device in devices:
        pl.semaphore_signal(barrier, inc=1, device_id=device, device_id_type=MESH)
    pl.semaphore_wait(barrier, len(devices))


def remote(source, target, sent, landed, device):
    return pltpu.make_async_remote_copy(
        src_ref=source,
        dst_ref=target,
        send_sem=sent,
        recv_sem=landed,
        device_id=device,
        device_id_type=MESH,
    )


def tensor_places():
    mine = lax.axis_index("tensor")
    return mine, mine + 1 - 2 * lax.rem(mine, 2), lax.rem(mine + 2, 4)


def scatter_kernel(
    rows, weights, own, weights_own, from_mate, from_partner, outgoing, arrived, t_sent, t_landed,
    w_sent, w_landed
):
    count, place = group_place()
    mine, mate, partner = tensor_places()
    beyond = lax.rem(mate + 2, 4)
    meet(
        [{"tensor": mate}, {"tensor": partner}]
        + [group_peer(step)[1] for step in range(1, count)]
    )
    first = remote(
        rows.at[beyond], from_mate.at[0], t_sent.at[0], t_landed.at[0], {"tensor": mate}
    )
    second = remote(rows.at[mate], from_mate.at[1], t_sent.at[1], t_landed.at[1], {"tensor": mate})
    first.start()
    second.start()
    copies = []
    for step in range(1, count):
        peer, device = group_peer(step)
        copies.append(
            remote(
                weights.at[peer],
                arrived.at[step - 1],
                w_sent.at[step - 1],
                w_landed.at[step - 1],
                device,
            )
        )
        copies[-1].start()
    first.wait()
    outgoing[...] = (
        rows[partner].astype(jnp.float32) + from_mate[0].astype(jnp.float32)
    ).astype(jnp.bfloat16)
    across = remote(outgoing, from_partner, t_sent.at[2], t_landed.at[2], {"tensor": partner})
    across.start()
    second.wait()
    own[...] = rows[mine].astype(jnp.float32) + from_mate[1].astype(jnp.float32)
    across.wait()
    own[...] = own[...] + from_partner[...].astype(jnp.float32)
    weights_own[...] = weights[place].astype(jnp.float32)
    for step in range(1, count):
        copies[step - 1].wait()
        weights_own[...] = weights_own[...] + arrived[step - 1].astype(jnp.float32)


def scatter_sums(rows, weights):
    _, length, width = rows.shape
    count, chunk, columns = weights.shape
    return pl.pallas_call(
        scatter_kernel,
        out_shape=(
            jax.ShapeDtypeStruct((length, width), jnp.float32),
            jax.ShapeDtypeStruct((chunk, columns), jnp.float32),
        ),
        in_specs=[IN_VMEM, IN_VMEM],
        out_specs=(IN_VMEM, IN_VMEM),
        scratch_shapes=[
            pltpu.VMEM((2, length, width), jnp.bfloat16),
            pltpu.VMEM((length, width), jnp.bfloat16),
            pltpu.VMEM((length, width), jnp.bfloat16),
            pltpu.VMEM((count - 1, chunk, columns), jnp.bfloat16),
            pltpu.SemaphoreType.DMA((3,)),
            pltpu.SemaphoreType.DMA((3,)),
            pltpu.SemaphoreType.DMA((count - 1,)),
            pltpu.SemaphoreType.DMA((count - 1,)),
        ],
        compiler_params=pltpu.CompilerParams(
            collective_id=1, has_side_effects=True, vmem_limit_bytes=40 * 2**20
        ),
    )(rows, weights)


def gather_kernel(
    own, weights, small, full, weights_sum, small_sum, w_arrived, s_arrived, w_part, s_part,
    w_tensor, s_tensor, t_sent, t_landed, g_sent, g_landed, h_sent, h_landed
):
    count, place = group_place()
    mine, mate, partner = tensor_places()
    others = [{"tensor": lax.rem(mine + step, 4)} for step in range(1, 4)]
    meet(others + [group_peer(step)[1] for step in range(1, count)])
    across = remote(own, full.at[mine], t_sent.at[0], t_landed.at[0], {"tensor": partner})
    aside = remote(own, full.at[mine], t_sent.at[1], t_landed.at[1], {"tensor": mate})
    copies = []
    for step in range(1, count):
        peer, device = group_peer(step)
        at = step - 1
        pair = (
            remote(small, s_arrived.at[at], g_sent.at[0, at], g_landed.at[0, at], device),
            remote(
                weights.at[peer], w_arrived.at[at], g_sent.at[1, at], g_landed.at[1, at], device
            ),
        )
        pair[0].start()
        pair[1].start()
        copies.append(pair)
    across.start()
    aside.start()
    full[pl.ds(mine, 1)] = own[...][None]
    s_part[...] = small[...]
    w_part[...] = weights[place].astype(jnp.float32)
    for step in range(1, count):
        for copy in copies[step - 1]:
            copy.wait()
        s_part[...] = s_part[...] + s_arrived[step - 1]
        w_part[...] = w_part[...] + w_arrived[step - 1].astype(jnp.float32)
    last = []
    for at, device in enumerate(others):
        last.append(
            (
                remote(s_part, s_tensor.at[at], h_sent.at[0, at], h_landed.at[0, at], device),
                remote(w_part, w_tensor.at[at], h_sent.at[1, at], h_landed.at[1, at], device),
            )
        )
        last[-1][0].start()
        last[-1][1].start()
    across.wait()
    onward = remote(
        full.at[partner], full.at[partner], t_sent.at[2], t_landed.at[2], {"tensor": mate}
    )
    onward.start()
    for pair in last:
        for copy in pair:
            copy.wait()
    whole = small.shape[0] // 2
    small_sum[...] = s_part[...]
    small_sum[pl.ds(0, whole)] = (
        s_part[pl.ds(0, whole)]
        + s_tensor[0, pl.ds(0, whole)]
        + s_tensor[1, pl.ds(0, whole)]
        + s_tensor[2, pl.ds(0, whole)]
    )
    weights_sum[...] = w_part[...] + w_tensor[0] + w_tensor[1] + w_tensor[2]
    aside.wait()
    onward.wait()


def gather_sums(own, weights, small):
    length, width = own.shape
    count, chunk, columns = weights.shape
    return pl.pallas_call(
        gather_kernel,
        out_shape=(
            jax.ShapeDtypeStruct((4, length, width), jnp.bfloat16),
            jax.ShapeDtypeStruct((chunk, columns), jnp.float32),
            jax.ShapeDtypeStruct(small.shape, jnp.float32),
        ),
        in_specs=[IN_VMEM, IN_VMEM, IN_VMEM],
        out_specs=(IN_VMEM, IN_VMEM, IN_VMEM),
        scratch_shapes=[
            pltpu.VMEM((count - 1, chunk, columns), jnp.bfloat16),
            pltpu.VMEM((count - 1,) + small.shape, jnp.float32),
            pltpu.VMEM((chunk, columns), jnp.float32),
            pltpu.VMEM(small.shape, jnp.float32),
            pltpu.VMEM((3, chunk, columns), jnp.float32),
            pltpu.VMEM((3,) + small.shape, jnp.float32),
            pltpu.SemaphoreType.DMA((3,)),
            pltpu.SemaphoreType.DMA((3,)),
            pltpu.SemaphoreType.DMA((2, count - 1)),
            pltpu.SemaphoreType.DMA((2, count - 1)),
            pltpu.SemaphoreType.DMA((2, 3)),
            pltpu.SemaphoreType.DMA((2, 3)),
        ],
        compiler_params=pltpu.CompilerParams(
            collective_id=2, has_side_effects=True, vmem_limit_bytes=40 * 2**20
        ),
    )(own, weights, small)


def on_device(
    tokens,
    norm_gain,
    w_z,
    w_x,
    w_bc,
    w_dt,
    conv_x,
    conv_bc,
    dt_bias,
    a_log,
    skip,
    gate_gain,
    w_out,
    cotangent,
):
    seq_count, span_len, model_width = tokens.shape
    row_count = seq_count * span_len
    head_count = dt_bias.shape[0]
    state_size = w_bc.shape[1] // 2
    tap_count = conv_x.shape[0]
    block_count = span_len // BLOCK
    inner_part = w_z.shape[1]
    packed = jnp.concatenate(
        [w_x, w_bc, jnp.pad(w_dt, ((0, 0), (0, 128 - head_count))), w_z, w_out.T], axis=1
    )
    full = lax.all_gather(packed, "shards", axis=0, tiled=True)
    at_z = inner_part + 2 * state_size + 128
    full_x = full[:, :inner_part]
    full_bc = full[:, inner_part : inner_part + 2 * state_size]
    full_dt = full[:, inner_part + 2 * state_size : inner_part + 2 * state_size + head_count]
    full_z = full[:, at_z : at_z + inner_part]
    out_t = full[:, at_z + inner_part :]
    inner_width = full_z.shape[1]
    head_width = inner_width // head_count
    flat_rows = tokens.reshape(row_count, model_width).astype(jnp.float32)
    row_scale = lax.rsqrt(jnp.mean(flat_rows * flat_rows, axis=1, keepdims=True) + epsilon)
    unit_rows = flat_rows * row_scale
    gain_input = norm_gain.astype(jnp.float32)
    normed = (unit_rows * gain_input).astype(jnp.bfloat16)
    fronts = product(normed, full[:, : at_z + inner_part])
    gate_value = fronts[:, at_z:]
    pre = fronts[:, : inner_part + 2 * state_size].astype(jnp.bfloat16)
    pre = pre.reshape(seq_count, span_len, inner_part + 2 * state_size)
    x_pre, bc_pre = pre[..., :inner_part], pre[..., inner_part:]
    dt_raw = fronts[:, inner_part + 2 * state_size : inner_part + 2 * state_size + head_count]
    edge = from_behind(pre[:, span_len - tap_count + 1 :], "context", 1)
    x_edge, bc_edge = edge[..., :inner_part], edge[..., inner_part:]
    x_conv, x_padded = depthwise(x_pre, x_edge, conv_x)
    bc_conv, bc_padded = depthwise(bc_pre, bc_edge, conv_bc)
    x_act = jax.nn.silu(x_conv).astype(jnp.bfloat16)
    bc_act = jax.nn.silu(bc_conv).astype(jnp.bfloat16)
    x_blocks = x_act.reshape(seq_count, block_count, BLOCK, head_count, head_width)
    b_in = bc_act[:, :, :state_size].reshape(seq_count, block_count, BLOCK, state_size)
    c_in = bc_act[:, :, state_size:].reshape(seq_count, block_count, BLOCK, state_size)
    pre_step = dt_raw + dt_bias
    step_size = jax.nn.softplus(pre_step)
    rate = -jnp.exp(a_log)
    step_heads = jnp.transpose(
        step_size.reshape(seq_count, block_count, BLOCK, head_count), (0, 1, 3, 2)
    )
    lower = jnp.tril(jnp.ones((BLOCK, BLOCK), jnp.float32))
    decay_sum = jnp.einsum("schj,ij->schi", step_heads * rate[:, None], lower, precision=highest)
    last_sum = decay_sum[..., -1]
    causal = lax.broadcasted_iota(jnp.int32, (BLOCK, BLOCK), 0) >= lax.broadcasted_iota(
        jnp.int32, (BLOCK, BLOCK), 1
    )
    gram_matrix = jnp.einsum("scin,scjn->scij", c_in, b_in, preferred_element_type=jnp.float32)
    spacing = decay_sum[..., :, None] - decay_sum[..., None, :]
    within = jnp.where(causal, jnp.exp(jnp.where(causal, spacing, 0.0)), 0.0)
    masked_within = within * step_heads[..., None, :]
    mix_full = gram_matrix[:, :, None] * masked_within
    mixing = mix_full.astype(jnp.bfloat16)
    intra = jnp.einsum("schij,scjhp->scihp", mixing, x_blocks, preferred_element_type=jnp.float32)
    toward = jnp.exp(last_sum[..., None] - decay_sum) * step_heads
    b_wide = b_in.astype(jnp.float32)
    loaded = (b_wide[:, :, None] * toward[..., None]).astype(jnp.bfloat16)
    fresh_state = jnp.einsum(
        "schjn,scjhp->schnp", loaded, x_blocks, preferred_element_type=jnp.float32
    )
    carried = jnp.zeros((seq_count, head_count, state_size, head_width), jnp.float32)
    entering = []
    for index in range(block_count):
        entering.append(carried)
        carried = jnp.exp(last_sum[:, index])[:, :, None, None] * carried + fresh_state[:, index]
    device_total = jnp.sum(last_sum, axis=1)
    device_decay = jnp.exp(device_total)
    incoming = from_behind(carried, "context", 1)
    after_sum = jnp.cumsum(last_sum, axis=1)
    start_decay = jnp.exp(after_sum - last_sum)
    enter_true = jnp.stack(entering, axis=1) + start_decay[..., None, None] * incoming[:, None]
    c_wide = c_in.astype(jnp.float32)
    reached = jnp.einsum("scin,schnp->scihp", c_wide, enter_true, precision=highest)
    growth = jnp.exp(jnp.transpose(decay_sum, (0, 1, 3, 2)))
    x_wide = x_blocks.astype(jnp.float32)
    scanned = intra + growth[..., None] * reached + skip[:, None] * x_wide
    scanned = scanned.reshape(row_count, inner_width)
    sigma_gate = jax.nn.sigmoid(gate_value)
    silu_gate = gate_value * sigma_gate
    gated_out = scanned * silu_gate
    gain_gate = gate_gain.astype(jnp.float32)
    weighted = (gated_out * gain_gate).astype(jnp.bfloat16)
    partial_value = product_transposed(weighted, out_t)
    square_sums = jnp.sum(gated_out * gated_out, axis=1)
    grad_rows = cotangent.reshape(row_count, model_width).astype(jnp.float32)
    scale_part = jnp.sum(grad_rows * partial_value, axis=1)
    squares, grad_scale = lax.psum(jnp.stack([square_sums, scale_part]), "tensor")
    own_rows = row_count // lax.axis_size("tensor")
    own_at = lax.axis_index("tensor") * own_rows

    def own(value):
        return lax.dynamic_slice_in_dim(value, own_at, own_rows, 0)

    out_scale = lax.rsqrt(squares / INNER + epsilon)
    own_projected = lax.psum_scatter(
        partial_value.astype(jnp.bfloat16), "tensor", scatter_dimension=0, tiled=True
    ).astype(jnp.float32)
    own_mixed = (own(flat_rows) + own_projected * own(out_scale)[:, None]).astype(jnp.bfloat16)
    mixed = lax.all_gather(own_mixed, "tensor", axis=0, tiled=True).reshape(tokens.shape)
    grad_spread = -0.5 * grad_scale * out_scale * out_scale * out_scale
    grad_proj = (grad_rows * out_scale[:, None]).astype(jnp.bfloat16)
    grad_weighted = product(grad_proj, out_t)
    grad_out_t = product_over_rows(grad_proj, weighted)
    grad_gate_gain = jnp.sum(grad_weighted * gated_out, axis=0)
    grad_gated = grad_weighted * gain_gate + 2.0 / INNER * grad_spread[:, None] * gated_out
    grad_scanned = (grad_gated * silu_gate).astype(jnp.bfloat16)
    grad_gate = (
        grad_gated * scanned * sigma_gate * (1.0 + gate_value * (1.0 - sigma_gate))
    ).astype(jnp.bfloat16)
    grad_w_z = product_over_rows(normed, grad_gate)
    grad_blocks = grad_scanned.reshape(seq_count, block_count, BLOCK, head_count, head_width)
    grad_wide = grad_blocks.astype(jnp.float32)
    grad_skip = jnp.sum(grad_wide * x_wide, axis=(0, 1, 2, 4))
    grad_reached = grad_wide * growth[..., None]
    from_output = jnp.einsum("scin,scihp->schnp", c_wide, grad_reached, precision=highest)
    carried_back = jnp.zeros_like(carried)
    leaving = []
    for index in range(block_count - 1, -1, -1):
        leaving.append(carried_back)
        carried_back = (
            from_output[:, index] + jnp.exp(last_sum[:, index])[:, :, None, None] * carried_back
        )
    outgoing = from_behind(carried_back, "context", -1)
    end_decay = jnp.exp(device_total[:, None] - after_sum)
    leave_true = jnp.stack(leaving[::-1], axis=1) + end_decay[..., None, None] * outgoing[:, None]
    grad_x_blocks = skip[:, None] * grad_wide
    grad_x_blocks = grad_x_blocks + jnp.einsum(
        "schij,scihp->scjhp", mixing, grad_blocks, preferred_element_type=jnp.float32
    )
    grad_x_blocks = grad_x_blocks + jnp.einsum(
        "schjn,schnp->scjhp", loaded.astype(jnp.float32), leave_true, precision=highest
    )
    grad_mix = jnp.einsum(
        "scihp,scjhp->schij", grad_blocks, x_blocks, preferred_element_type=jnp.float32
    )
    grad_gram = jnp.sum(grad_mix * masked_within, axis=2)
    grad_step = jnp.sum(grad_mix * gram_matrix[:, :, None] * within, axis=3)
    spread_term = grad_mix * mix_full
    grad_cum = jnp.sum(spread_term, axis=4) - jnp.sum(spread_term, axis=3)
    grad_c_in = jnp.einsum("scij,scjn->scin", grad_gram, b_wide, precision=highest)
    grad_c_in = grad_c_in + jnp.einsum(
        "scihp,schnp->scin", grad_reached, enter_true, precision=highest
    )
    grad_b_in = jnp.einsum("scij,scin->scjn", grad_gram, c_wide, precision=highest)
    grad_cum = grad_cum + jnp.transpose(jnp.sum(grad_reached * reached, axis=4), (0, 1, 3, 2))
    grad_last = jnp.sum(leave_true * enter_true, axis=(3, 4)) * jnp.exp(last_sum)
    grad_loaded = jnp.einsum("scjhp,schnp->schjn", x_wide, leave_true, precision=highest)
    grad_b_in = grad_b_in + jnp.sum(grad_loaded * toward[..., None], axis=2)
    touch = jnp.sum(grad_loaded * b_wide[:, :, None], axis=4)
    touch_part = touch * toward
    grad_step = grad_step + touch * jnp.exp(last_sum[..., None] - decay_sum)
    grad_last = grad_last + jnp.sum(touch_part, axis=3)
    grad_cum = (grad_cum - touch_part).at[..., -1].add(grad_last)
    grad_log = jnp.einsum("schi,ij->schj", grad_cum, lower, precision=highest)
    grad_step = grad_step + grad_log * rate[:, None]
    grad_a_log = jnp.sum(grad_log * step_heads, axis=(0, 1, 3)) * rate
    grad_pre = jnp.transpose(grad_step, (0, 1, 3, 2)).reshape(
        row_count, head_count
    ) * jax.nn.sigmoid(pre_step)
    grad_dt_bias = jnp.sum(grad_pre, axis=0)
    grad_dt_raw = grad_pre.astype(jnp.bfloat16)
    grad_x_conv = grad_x_blocks.reshape(seq_count, span_len, inner_width) * silu_slope(x_conv)
    grad_bc_act = jnp.concatenate([grad_b_in, grad_c_in], axis=3).reshape(
        seq_count, span_len, 2 * state_size
    )
    grad_bc_conv = grad_bc_act * silu_slope(bc_conv)
    following = from_behind(
        jnp.concatenate(
            [grad_x_conv[:, : tap_count - 1], grad_bc_conv[:, : tap_count - 1]], axis=2
        ),
        "context",
        -1,
    )
    x_next, bc_next = following[..., :inner_width], following[..., inner_width:]
    grad_x_signal, grad_conv_x = depthwise_back(grad_x_conv, x_next, conv_x, x_padded)
    grad_bc_signal, conv_bc_part = depthwise_back(grad_bc_conv, bc_next, conv_bc, bc_padded)
    grad_x_pre = grad_x_signal.reshape(row_count, inner_width).astype(jnp.bfloat16)
    normed_part = (
        product_transposed(grad_gate, full_z)
        + product_transposed(grad_x_pre, full_x)
        + product_transposed(grad_dt_raw, full_dt)
    )
    group_count = group_place()[0]
    grad_w_x = product_over_rows(normed, grad_x_pre)
    grad_w_dt = product_over_rows(normed, grad_dt_raw)
    rows_all = jnp.concatenate(
        [normed_part, grad_bc_signal.reshape(row_count, 2 * state_size)], axis=1
    ).astype(jnp.bfloat16)
    grads_all = jnp.concatenate(
        [grad_w_x, grad_w_z, grad_out_t, jnp.pad(grad_w_dt, ((0, 0), (0, 128 - head_count)))],
        axis=1,
    ).astype(jnp.bfloat16)
    own_sums, final_all = scatter_sums(
        rows_all.reshape(4, own_rows, -1), grads_all.reshape(group_count, -1, grads_all.shape[1])
    )
    own_grad = own_sums[:, :model_width]
    own_bc = own_sums[:, model_width:].astype(jnp.bfloat16)
    final_x = final_all[:, :inner_width]
    final_z = final_all[:, inner_width : 2 * inner_width]
    final_out = final_all[:, 2 * inner_width : 3 * inner_width].T
    final_dt = final_all[:, 3 * inner_width : 3 * inner_width + head_count]
    own_grad = own_grad + product_transposed(own_bc, full_bc)
    own_unit = own(unit_rows)
    grad_norm_gain = jnp.sum(own_grad * own_unit, axis=0)
    grad_unit = own_grad * gain_input
    own_tokens = own(grad_rows) + own(row_scale) * (
        grad_unit - own_unit * jnp.mean(grad_unit * own_unit, axis=1, keepdims=True)
    )
    grad_w_bc = product_over_rows(own(normed), own_bc).astype(jnp.bfloat16)
    whole = jnp.concatenate([grad_norm_gain, conv_bc_part.reshape(-1)])
    by_tensor = jnp.concatenate(
        [grad_conv_x.reshape(-1), grad_gate_gain, grad_dt_bias, grad_a_log, grad_skip]
    )
    half = -(-max(whole.shape[0], by_tensor.shape[0]) // 1024) * 1024
    small = jnp.concatenate(
        [
            jnp.pad(whole, (0, half - whole.shape[0])),
            jnp.pad(by_tensor, (0, half - by_tensor.shape[0])),
        ]
    ).reshape(-1, 128)
    gathered, final_bc, sums = gather_sums(
        own_tokens.astype(jnp.bfloat16), grad_w_bc.reshape(group_count, -1, 2 * state_size), small
    )
    grad_tokens = gathered.astype(jnp.float32)
    sums = sums.reshape(2, half)
    norm_sum = sums[0, :model_width]
    conv_bc_sum = sums[0, model_width : whole.shape[0]].reshape(conv_bc.shape)
    mine = sums[1, : by_tensor.shape[0]]
    at = tap_count * inner_width
    conv_x_sum = mine[:at].reshape(tap_count, inner_width)
    gate_gain_sum = mine[at : at + inner_width]
    heads_sum = mine[at + inner_width :].reshape(3, head_count)
    return (
        mixed,
        grad_tokens.reshape(seq_count, span_len, model_width),
        norm_sum,
        final_z,
        final_x,
        final_bc,
        final_dt,
        conv_x_sum,
        conv_bc_sum,
        heads_sum[0],
        heads_sum[1],
        heads_sum[2],
        gate_gain_sum,
        final_out,
    )


def solution(mesh):
    placed = (
        P("shards", "context", None),
        P(),
        P("shards", "tensor"),
        P("shards", "tensor"),
        P("shards", None),
        P("shards", "tensor"),
        P(None, "tensor"),
        P(),
        P("tensor"),
        P("tensor"),
        P("tensor"),
        P("tensor"),
        P("tensor", "shards"),
        P("shards", "context", None),
    )
    return jax.shard_map(
        on_device,
        mesh=mesh,
        in_specs=placed,
        out_specs=(
            P("shards", "context", None),
            P("shards", "context", None),
            P(),
            P(("shards", "context"), "tensor"),
            P(("shards", "context"), "tensor"),
            P(("shards", "context"), None),
            P(("shards", "context"), "tensor"),
            P(None, "tensor"),
            P(),
            P("tensor"),
            P("tensor"),
            P("tensor"),
            P("tensor"),
            P("tensor", ("shards", "context")),
        ),
        check_vma=False,
    )
```

```python
import jax
import jax.numpy as jnp
from jax import lax
from jax.experimental import pallas as pl
from jax.experimental.pallas import tpu as pltpu
from jax.sharding import PartitionSpec as P

BLOCK = 256
INNER = 1536


epsilon = 1e-05
highest = lax.Precision.HIGHEST


def from_behind(value, axis, steps):
    count = lax.axis_size(axis)
    first, last = (max(0, -steps), min(count, count - steps))
    return lax.ppermute(value, axis, [(source, source + steps) for source in range(first, last)])


def product(left, right):
    return jnp.dot(left, right, preferred_element_type=jnp.float32)


def product_transposed(left, right):
    return lax.dot_general(
        left, right, (((1,), (1,)), ((), ())), preferred_element_type=jnp.float32
    )


def product_over_rows(left, right):
    return lax.dot_general(
        left, right, (((0,), (0,)), ((), ())), preferred_element_type=jnp.float32
    )


def depthwise(signal, edge_rows, weights):
    tap_count = weights.shape[0]
    span_len = signal.shape[1]
    padded = jnp.concatenate([edge_rows, signal], axis=1).astype(jnp.float32)
    wide_taps = weights.astype(jnp.float32)
    total = wide_taps[0] * padded[:, 0:span_len]
    for offset in range(1, tap_count):
        total = total + wide_taps[offset] * padded[:, offset : offset + span_len]
    return (total, padded)


def depthwise_back(grad_conv, edge_rows, weights, padded):
    tap_count = weights.shape[0]
    span_len = grad_conv.shape[1]
    wide_taps = weights.astype(jnp.float32)
    extended = jnp.concatenate([grad_conv, edge_rows], axis=1)
    grad_signal = wide_taps[tap_count - 1] * extended[:, 0:span_len]
    for offset in range(1, tap_count):
        grad_signal = (
            grad_signal
            + wide_taps[tap_count - 1 - offset] * extended[:, offset : offset + span_len]
        )
    grad_taps = jnp.stack(
        [
            jnp.sum(grad_conv * padded[:, offset : offset + span_len], axis=(0, 1))
            for offset in range(tap_count)
        ]
    )
    return (grad_signal, grad_taps)


def silu_slope(value):
    sigma = jax.nn.sigmoid(value)
    return sigma * (1.0 + value * (1.0 - sigma))


MESH = pl.DeviceIdType.MESH
IN_VMEM = pl.BlockSpec(memory_space=pltpu.VMEM)


def group_place():
    places = lax.axis_size("context")
    count = lax.axis_size("shards") * places
    mine = lax.axis_index("shards") * places + lax.axis_index("context")
    return count, mine


def group_peer(steps):
    count, mine = group_place()
    peer = lax.rem(mine + steps, count)
    places = lax.axis_size("context")
    return peer, {"shards": peer // places, "context": lax.rem(peer, places)}


def meet(devices):
    barrier = pltpu.get_barrier_semaphore()
    for device in devices:
        pl.semaphore_signal(barrier, inc=1, device_id=device, device_id_type=MESH)
    pl.semaphore_wait(barrier, len(devices))


def remote(source, target, sent, landed, device):
    return pltpu.make_async_remote_copy(
        src_ref=source,
        dst_ref=target,
        send_sem=sent,
        recv_sem=landed,
        device_id=device,
        device_id_type=MESH,
    )


def tensor_places():
    mine = lax.axis_index("tensor")
    return mine, mine + 1 - 2 * lax.rem(mine, 2), lax.rem(mine + 2, 4)


def scatter_kernel(
    rows, weights, own, weights_own, from_mate, from_partner, outgoing, arrived, t_sent, t_landed,
    w_sent, w_landed
):
    count, place = group_place()
    mine, mate, partner = tensor_places()
    beyond = lax.rem(mate + 2, 4)
    meet(
        [{"tensor": mate}, {"tensor": partner}]
        + [group_peer(step)[1] for step in range(1, count)]
    )
    first = remote(
        rows.at[beyond], from_mate.at[0], t_sent.at[0], t_landed.at[0], {"tensor": mate}
    )
    second = remote(rows.at[mate], from_mate.at[1], t_sent.at[1], t_landed.at[1], {"tensor": mate})
    first.start()
    second.start()
    copies = []
    for step in range(1, count):
        peer, device = group_peer(step)
        copies.append(
            remote(
                weights.at[peer],
                arrived.at[step - 1],
                w_sent.at[step - 1],
                w_landed.at[step - 1],
                device,
            )
        )
        copies[-1].start()
    first.wait()
    outgoing[...] = (
        rows[partner].astype(jnp.float32) + from_mate[0].astype(jnp.float32)
    ).astype(jnp.bfloat16)
    across = remote(outgoing, from_partner, t_sent.at[2], t_landed.at[2], {"tensor": partner})
    across.start()
    second.wait()
    own[...] = rows[mine].astype(jnp.float32) + from_mate[1].astype(jnp.float32)
    across.wait()
    own[...] = own[...] + from_partner[...].astype(jnp.float32)
    weights_own[...] = weights[place].astype(jnp.float32)
    for step in range(1, count):
        copies[step - 1].wait()
        weights_own[...] = weights_own[...] + arrived[step - 1].astype(jnp.float32)


def scatter_sums(rows, weights):
    _, length, width = rows.shape
    count, chunk, columns = weights.shape
    return pl.pallas_call(
        scatter_kernel,
        out_shape=(
            jax.ShapeDtypeStruct((length, width), jnp.float32),
            jax.ShapeDtypeStruct((chunk, columns), jnp.float32),
        ),
        in_specs=[IN_VMEM, IN_VMEM],
        out_specs=(IN_VMEM, IN_VMEM),
        scratch_shapes=[
            pltpu.VMEM((2, length, width), jnp.bfloat16),
            pltpu.VMEM((length, width), jnp.bfloat16),
            pltpu.VMEM((length, width), jnp.bfloat16),
            pltpu.VMEM((count - 1, chunk, columns), jnp.bfloat16),
            pltpu.SemaphoreType.DMA((3,)),
            pltpu.SemaphoreType.DMA((3,)),
            pltpu.SemaphoreType.DMA((count - 1,)),
            pltpu.SemaphoreType.DMA((count - 1,)),
        ],
        compiler_params=pltpu.CompilerParams(
            collective_id=1, has_side_effects=True, vmem_limit_bytes=40 * 2**20
        ),
    )(rows, weights)


def gather_kernel(
    own, weights, small, full, weights_sum, small_sum, w_arrived, s_arrived, w_part, s_part,
    w_tensor, s_tensor, t_sent, t_landed, g_sent, g_landed, h_sent, h_landed
):
    count, place = group_place()
    mine, mate, partner = tensor_places()
    others = [{"tensor": lax.rem(mine + step, 4)} for step in range(1, 4)]
    meet(others + [group_peer(step)[1] for step in range(1, count)])
    across = remote(own, full.at[mine], t_sent.at[0], t_landed.at[0], {"tensor": partner})
    aside = remote(own, full.at[mine], t_sent.at[1], t_landed.at[1], {"tensor": mate})
    across.start()
    aside.start()
    copies = []
    for step in range(1, count):
        peer, device = group_peer(step)
        at = step - 1
        pair = (
            remote(small, s_arrived.at[at], g_sent.at[0, at], g_landed.at[0, at], device),
            remote(
                weights.at[peer], w_arrived.at[at], g_sent.at[1, at], g_landed.at[1, at], device
            ),
        )
        pair[0].start()
        pair[1].start()
        copies.append(pair)
    full[pl.ds(mine, 1)] = own[...][None]
    s_part[...] = small[...]
    w_part[...] = weights[place].astype(jnp.float32)
    for step in range(1, count):
        for copy in copies[step - 1]:
            copy.wait()
        s_part[...] = s_part[...] + s_arrived[step - 1]
        w_part[...] = w_part[...] + w_arrived[step - 1].astype(jnp.float32)
    last = []
    for at, device in enumerate(others):
        last.append(
            (
                remote(s_part, s_tensor.at[at], h_sent.at[0, at], h_landed.at[0, at], device),
                remote(w_part, w_tensor.at[at], h_sent.at[1, at], h_landed.at[1, at], device),
            )
        )
        last[-1][0].start()
        last[-1][1].start()
    across.wait()
    onward = remote(
        full.at[partner], full.at[partner], t_sent.at[2], t_landed.at[2], {"tensor": mate}
    )
    onward.start()
    for pair in last:
        for copy in pair:
            copy.wait()
    whole = small.shape[0] // 2
    small_sum[...] = s_part[...]
    small_sum[pl.ds(0, whole)] = (
        s_part[pl.ds(0, whole)]
        + s_tensor[0, pl.ds(0, whole)]
        + s_tensor[1, pl.ds(0, whole)]
        + s_tensor[2, pl.ds(0, whole)]
    )
    weights_sum[...] = w_part[...] + w_tensor[0] + w_tensor[1] + w_tensor[2]
    aside.wait()
    onward.wait()


def gather_sums(own, weights, small):
    length, width = own.shape
    count, chunk, columns = weights.shape
    return pl.pallas_call(
        gather_kernel,
        out_shape=(
            jax.ShapeDtypeStruct((4, length, width), jnp.bfloat16),
            jax.ShapeDtypeStruct((chunk, columns), jnp.float32),
            jax.ShapeDtypeStruct(small.shape, jnp.float32),
        ),
        in_specs=[IN_VMEM, IN_VMEM, IN_VMEM],
        out_specs=(IN_VMEM, IN_VMEM, IN_VMEM),
        scratch_shapes=[
            pltpu.VMEM((count - 1, chunk, columns), jnp.bfloat16),
            pltpu.VMEM((count - 1,) + small.shape, jnp.float32),
            pltpu.VMEM((chunk, columns), jnp.float32),
            pltpu.VMEM(small.shape, jnp.float32),
            pltpu.VMEM((3, chunk, columns), jnp.float32),
            pltpu.VMEM((3,) + small.shape, jnp.float32),
            pltpu.SemaphoreType.DMA((3,)),
            pltpu.SemaphoreType.DMA((3,)),
            pltpu.SemaphoreType.DMA((2, count - 1)),
            pltpu.SemaphoreType.DMA((2, count - 1)),
            pltpu.SemaphoreType.DMA((2, 3)),
            pltpu.SemaphoreType.DMA((2, 3)),
        ],
        compiler_params=pltpu.CompilerParams(
            collective_id=2, has_side_effects=True, vmem_limit_bytes=40 * 2**20
        ),
    )(own, weights, small)


def on_device(
    tokens,
    norm_gain,
    w_z,
    w_x,
    w_bc,
    w_dt,
    conv_x,
    conv_bc,
    dt_bias,
    a_log,
    skip,
    gate_gain,
    w_out,
    cotangent,
):
    seq_count, span_len, model_width = tokens.shape
    row_count = seq_count * span_len
    head_count = dt_bias.shape[0]
    state_size = w_bc.shape[1] // 2
    tap_count = conv_x.shape[0]
    block_count = span_len // BLOCK
    inner_part = w_z.shape[1]
    packed = jnp.concatenate(
        [w_x, w_bc, jnp.pad(w_dt, ((0, 0), (0, 128 - head_count))), w_z, w_out.T], axis=1
    )
    full = lax.all_gather(packed, "shards", axis=0, tiled=True)
    at_z = inner_part + 2 * state_size + 128
    full_x = full[:, :inner_part]
    full_bc = full[:, inner_part : inner_part + 2 * state_size]
    full_dt = full[:, inner_part + 2 * state_size : inner_part + 2 * state_size + head_count]
    full_z = full[:, at_z : at_z + inner_part]
    out_t = full[:, at_z + inner_part :]
    inner_width = full_z.shape[1]
    head_width = inner_width // head_count
    flat_rows = tokens.reshape(row_count, model_width).astype(jnp.float32)
    row_scale = lax.rsqrt(jnp.mean(flat_rows * flat_rows, axis=1, keepdims=True) + epsilon)
    unit_rows = flat_rows * row_scale
    gain_input = norm_gain.astype(jnp.float32)
    normed = (unit_rows * gain_input).astype(jnp.bfloat16)
    fronts = product(normed, full[:, : at_z + inner_part])
    gate_value = fronts[:, at_z:]
    pre = fronts[:, : inner_part + 2 * state_size].astype(jnp.bfloat16)
    pre = pre.reshape(seq_count, span_len, inner_part + 2 * state_size)
    x_pre, bc_pre = pre[..., :inner_part], pre[..., inner_part:]
    dt_raw = fronts[:, inner_part + 2 * state_size : inner_part + 2 * state_size + head_count]
    edge = from_behind(pre[:, span_len - tap_count + 1 :], "context", 1)
    x_edge, bc_edge = edge[..., :inner_part], edge[..., inner_part:]
    x_conv, x_padded = depthwise(x_pre, x_edge, conv_x)
    bc_conv, bc_padded = depthwise(bc_pre, bc_edge, conv_bc)
    x_act = jax.nn.silu(x_conv).astype(jnp.bfloat16)
    bc_act = jax.nn.silu(bc_conv).astype(jnp.bfloat16)
    x_blocks = x_act.reshape(seq_count, block_count, BLOCK, head_count, head_width)
    b_in = bc_act[:, :, :state_size].reshape(seq_count, block_count, BLOCK, state_size)
    c_in = bc_act[:, :, state_size:].reshape(seq_count, block_count, BLOCK, state_size)
    pre_step = dt_raw + dt_bias
    step_size = jax.nn.softplus(pre_step)
    rate = -jnp.exp(a_log)
    step_heads = jnp.transpose(
        step_size.reshape(seq_count, block_count, BLOCK, head_count), (0, 1, 3, 2)
    )
    lower = jnp.tril(jnp.ones((BLOCK, BLOCK), jnp.float32))
    decay_sum = jnp.einsum("schj,ij->schi", step_heads * rate[:, None], lower, precision=highest)
    last_sum = decay_sum[..., -1]
    causal = lax.broadcasted_iota(jnp.int32, (BLOCK, BLOCK), 0) >= lax.broadcasted_iota(
        jnp.int32, (BLOCK, BLOCK), 1
    )
    gram_matrix = jnp.einsum("scin,scjn->scij", c_in, b_in, preferred_element_type=jnp.float32)
    spacing = decay_sum[..., :, None] - decay_sum[..., None, :]
    within = jnp.where(causal, jnp.exp(jnp.where(causal, spacing, 0.0)), 0.0)
    masked_within = within * step_heads[..., None, :]
    mix_full = gram_matrix[:, :, None] * masked_within
    mixing = mix_full.astype(jnp.bfloat16)
    intra = jnp.einsum("schij,scjhp->scihp", mixing, x_blocks, preferred_element_type=jnp.float32)
    toward = jnp.exp(last_sum[..., None] - decay_sum) * step_heads
    b_wide = b_in.astype(jnp.float32)
    loaded = (b_wide[:, :, None] * toward[..., None]).astype(jnp.bfloat16)
    fresh_state = jnp.einsum(
        "schjn,scjhp->schnp", loaded, x_blocks, preferred_element_type=jnp.float32
    )
    carried = jnp.zeros((seq_count, head_count, state_size, head_width), jnp.float32)
    entering = []
    for index in range(block_count):
        entering.append(carried)
        carried = jnp.exp(last_sum[:, index])[:, :, None, None] * carried + fresh_state[:, index]
    device_total = jnp.sum(last_sum, axis=1)
    device_decay = jnp.exp(device_total)
    incoming = from_behind(carried.astype(jnp.bfloat16), "context", 1).astype(jnp.float32)
    after_sum = jnp.cumsum(last_sum, axis=1)
    start_decay = jnp.exp(after_sum - last_sum)
    enter_true = jnp.stack(entering, axis=1) + start_decay[..., None, None] * incoming[:, None]
    enter_low = enter_true.astype(jnp.bfloat16)
    reached = jnp.einsum("scin,schnp->scihp", c_in, enter_low, preferred_element_type=jnp.float32)
    growth = jnp.exp(jnp.transpose(decay_sum, (0, 1, 3, 2)))
    x_wide = x_blocks.astype(jnp.float32)
    scanned = intra + growth[..., None] * reached + skip[:, None] * x_wide
    scanned = scanned.reshape(row_count, inner_width)
    sigma_gate = jax.nn.sigmoid(gate_value)
    silu_gate = gate_value * sigma_gate
    gated_out = scanned * silu_gate
    gain_gate = gate_gain.astype(jnp.float32)
    weighted = (gated_out * gain_gate).astype(jnp.bfloat16)
    partial_value = product_transposed(weighted, out_t)
    square_sums = jnp.sum(gated_out * gated_out, axis=1)
    grad_rows = cotangent.reshape(row_count, model_width).astype(jnp.float32)
    scale_part = jnp.sum(grad_rows * partial_value, axis=1)
    squares, grad_scale = lax.psum(jnp.stack([square_sums, scale_part]), "tensor")
    own_rows = row_count // lax.axis_size("tensor")
    own_at = lax.axis_index("tensor") * own_rows

    def own(value):
        return lax.dynamic_slice_in_dim(value, own_at, own_rows, 0)

    out_scale = lax.rsqrt(squares / INNER + epsilon)
    own_projected = lax.psum_scatter(
        partial_value.astype(jnp.bfloat16), "tensor", scatter_dimension=0, tiled=True
    ).astype(jnp.float32)
    own_mixed = (own(flat_rows) + own_projected * own(out_scale)[:, None]).astype(jnp.bfloat16)
    mixed = lax.all_gather(own_mixed, "tensor", axis=0, tiled=True).reshape(tokens.shape)
    grad_spread = -0.5 * grad_scale * out_scale * out_scale * out_scale
    grad_proj = (grad_rows * out_scale[:, None]).astype(jnp.bfloat16)
    grad_weighted = product(grad_proj, out_t)
    grad_out_t = product_over_rows(grad_proj, weighted)
    grad_gate_gain = jnp.sum(grad_weighted * gated_out, axis=0)
    grad_gated = grad_weighted * gain_gate + 2.0 / INNER * grad_spread[:, None] * gated_out
    grad_scanned = (grad_gated * silu_gate).astype(jnp.bfloat16)
    grad_gate = (
        grad_gated * scanned * sigma_gate * (1.0 + gate_value * (1.0 - sigma_gate))
    ).astype(jnp.bfloat16)
    grad_w_z = product_over_rows(normed, grad_gate)
    grad_blocks = grad_scanned.reshape(seq_count, block_count, BLOCK, head_count, head_width)
    grad_wide = grad_blocks.astype(jnp.float32)
    grad_skip = jnp.sum(grad_wide * x_wide, axis=(0, 1, 2, 4))
    grad_reached = grad_wide * growth[..., None]
    reached_low = grad_reached.astype(jnp.bfloat16)
    from_output = jnp.einsum("scin,scihp->schnp", c_in, reached_low, preferred_element_type=jnp.float32)
    carried_back = jnp.zeros_like(carried)
    leaving = []
    for index in range(block_count - 1, -1, -1):
        leaving.append(carried_back)
        carried_back = (
            from_output[:, index] + jnp.exp(last_sum[:, index])[:, :, None, None] * carried_back
        )
    outgoing = from_behind(carried_back.astype(jnp.bfloat16), "context", -1).astype(jnp.float32)
    end_decay = jnp.exp(device_total[:, None] - after_sum)
    leave_true = jnp.stack(leaving[::-1], axis=1) + end_decay[..., None, None] * outgoing[:, None]
    leave_low = leave_true.astype(jnp.bfloat16)
    grad_x_blocks = skip[:, None] * grad_wide
    grad_x_blocks = grad_x_blocks + jnp.einsum(
        "schij,scihp->scjhp", mixing, grad_blocks, preferred_element_type=jnp.float32
    )
    grad_x_blocks = grad_x_blocks + jnp.einsum(
        "schjn,schnp->scjhp", loaded, leave_low, preferred_element_type=jnp.float32
    )
    grad_mix = jnp.einsum(
        "scihp,scjhp->schij", grad_blocks, x_blocks, preferred_element_type=jnp.float32
    )
    grad_gram = jnp.sum(grad_mix * masked_within, axis=2).astype(jnp.bfloat16)
    grad_step = jnp.sum(grad_mix * gram_matrix[:, :, None] * within, axis=3)
    spread_term = grad_mix * mix_full
    grad_cum = jnp.sum(spread_term, axis=4) - jnp.sum(spread_term, axis=3)
    grad_c_in = jnp.einsum("scij,scjn->scin", grad_gram, b_in, preferred_element_type=jnp.float32)
    grad_c_in = grad_c_in + jnp.einsum(
        "scihp,schnp->scin", reached_low, enter_low, preferred_element_type=jnp.float32
    )
    grad_b_in = jnp.einsum("scij,scin->scjn", grad_gram, c_in, preferred_element_type=jnp.float32)
    grad_cum = grad_cum + jnp.transpose(jnp.sum(grad_reached * reached, axis=4), (0, 1, 3, 2))
    grad_last = jnp.sum(leave_true * enter_true, axis=(3, 4)) * jnp.exp(last_sum)
    grad_loaded = jnp.einsum("scjhp,schnp->schjn", x_blocks, leave_low, preferred_element_type=jnp.float32)
    grad_b_in = grad_b_in + jnp.sum(grad_loaded * toward[..., None], axis=2)
    touch = jnp.sum(grad_loaded * b_wide[:, :, None], axis=4)
    touch_part = touch * toward
    grad_step = grad_step + touch * jnp.exp(last_sum[..., None] - decay_sum)
    grad_last = grad_last + jnp.sum(touch_part, axis=3)
    grad_cum = (grad_cum - touch_part).at[..., -1].add(grad_last)
    grad_log = jnp.einsum("schi,ij->schj", grad_cum, lower, precision=highest)
    grad_step = grad_step + grad_log * rate[:, None]
    grad_a_log = jnp.sum(grad_log * step_heads, axis=(0, 1, 3)) * rate
    grad_pre = jnp.transpose(grad_step, (0, 1, 3, 2)).reshape(
        row_count, head_count
    ) * jax.nn.sigmoid(pre_step)
    grad_dt_bias = jnp.sum(grad_pre, axis=0)
    grad_dt_raw = grad_pre.astype(jnp.bfloat16)
    grad_x_conv = grad_x_blocks.reshape(seq_count, span_len, inner_width) * silu_slope(x_conv)
    grad_bc_act = jnp.concatenate([grad_b_in, grad_c_in], axis=3).reshape(
        seq_count, span_len, 2 * state_size
    )
    grad_bc_conv = grad_bc_act * silu_slope(bc_conv)
    following = from_behind(
        jnp.concatenate(
            [grad_x_conv[:, : tap_count - 1], grad_bc_conv[:, : tap_count - 1]], axis=2
        ),
        "context",
        -1,
    )
    x_next, bc_next = following[..., :inner_width], following[..., inner_width:]
    grad_x_signal, grad_conv_x = depthwise_back(grad_x_conv, x_next, conv_x, x_padded)
    grad_bc_signal, conv_bc_part = depthwise_back(grad_bc_conv, bc_next, conv_bc, bc_padded)
    grad_x_pre = grad_x_signal.reshape(row_count, inner_width).astype(jnp.bfloat16)
    normed_part = (
        product_transposed(grad_gate, full_z)
        + product_transposed(grad_x_pre, full_x)
        + product_transposed(grad_dt_raw, full_dt)
    )
    group_count = group_place()[0]
    grad_w_x = product_over_rows(normed, grad_x_pre)
    grad_w_dt = product_over_rows(normed, grad_dt_raw)
    rows_all = jnp.concatenate(
        [normed_part, grad_bc_signal.reshape(row_count, 2 * state_size)], axis=1
    ).astype(jnp.bfloat16)
    grads_all = jnp.concatenate(
        [grad_w_x, grad_w_z, grad_out_t, jnp.pad(grad_w_dt, ((0, 0), (0, 128 - head_count)))],
        axis=1,
    ).astype(jnp.bfloat16)
    own_sums, final_all = scatter_sums(
        rows_all.reshape(4, own_rows, -1), grads_all.reshape(group_count, -1, grads_all.shape[1])
    )
    own_grad = own_sums[:, :model_width]
    own_bc = own_sums[:, model_width:].astype(jnp.bfloat16)
    final_x = final_all[:, :inner_width]
    final_z = final_all[:, inner_width : 2 * inner_width]
    final_out = final_all[:, 2 * inner_width : 3 * inner_width].T
    final_dt = final_all[:, 3 * inner_width : 3 * inner_width + head_count]
    own_grad = own_grad + product_transposed(own_bc, full_bc)
    own_unit = own(unit_rows)
    grad_norm_gain = jnp.sum(own_grad * own_unit, axis=0)
    grad_unit = own_grad * gain_input
    own_tokens = own(grad_rows) + own(row_scale) * (
        grad_unit - own_unit * jnp.mean(grad_unit * own_unit, axis=1, keepdims=True)
    )
    grad_w_bc = product_over_rows(own(normed), own_bc).astype(jnp.bfloat16)
    whole = jnp.concatenate([grad_norm_gain, conv_bc_part.reshape(-1)])
    by_tensor = jnp.concatenate(
        [grad_conv_x.reshape(-1), grad_gate_gain, grad_dt_bias, grad_a_log, grad_skip]
    )
    half = -(-max(whole.shape[0], by_tensor.shape[0]) // 1024) * 1024
    small = jnp.concatenate(
        [
            jnp.pad(whole, (0, half - whole.shape[0])),
            jnp.pad(by_tensor, (0, half - by_tensor.shape[0])),
        ]
    ).reshape(-1, 128)
    gathered, final_bc, sums = gather_sums(
        own_tokens.astype(jnp.bfloat16), grad_w_bc.reshape(group_count, -1, 2 * state_size), small
    )
    grad_tokens = gathered.astype(jnp.float32)
    sums = sums.reshape(2, half)
    norm_sum = sums[0, :model_width]
    conv_bc_sum = sums[0, model_width : whole.shape[0]].reshape(conv_bc.shape)
    mine = sums[1, : by_tensor.shape[0]]
    at = tap_count * inner_width
    conv_x_sum = mine[:at].reshape(tap_count, inner_width)
    gate_gain_sum = mine[at : at + inner_width]
    heads_sum = mine[at + inner_width :].reshape(3, head_count)
    return (
        mixed,
        grad_tokens.reshape(seq_count, span_len, model_width),
        norm_sum,
        final_z,
        final_x,
        final_bc,
        final_dt,
        conv_x_sum,
        conv_bc_sum,
        heads_sum[0],
        heads_sum[1],
        heads_sum[2],
        gate_gain_sum,
        final_out,
    )


def solution(mesh):
    placed = (
        P("shards", "context", None),
        P(),
        P("shards", "tensor"),
        P("shards", "tensor"),
        P("shards", None),
        P("shards", "tensor"),
        P(None, "tensor"),
        P(),
        P("tensor"),
        P("tensor"),
        P("tensor"),
        P("tensor"),
        P("tensor", "shards"),
        P("shards", "context", None),
    )
    return jax.shard_map(
        on_device,
        mesh=mesh,
        in_specs=placed,
        out_specs=(
            P("shards", "context", None),
            P("shards", "context", None),
            P(),
            P(("shards", "context"), "tensor"),
            P(("shards", "context"), "tensor"),
            P(("shards", "context"), None),
            P(("shards", "context"), "tensor"),
            P(None, "tensor"),
            P(),
            P("tensor"),
            P("tensor"),
            P("tensor"),
            P("tensor"),
            P("tensor", ("shards", "context")),
        ),
        check_vma=False,
    )
```

```python
import jax
import jax.numpy as jnp
from jax import lax
from jax.experimental import pallas as pl
from jax.experimental.pallas import tpu as pltpu
from jax.sharding import PartitionSpec as P

BLOCK = 256
INNER = 1536


epsilon = 1e-05
highest = lax.Precision.HIGHEST


def from_behind(value, axis, steps):
    count = lax.axis_size(axis)
    first, last = (max(0, -steps), min(count, count - steps))
    return lax.ppermute(value, axis, [(source, source + steps) for source in range(first, last)])


def product(left, right):
    return jnp.dot(left, right, preferred_element_type=jnp.float32)


def product_transposed(left, right):
    return lax.dot_general(
        left, right, (((1,), (1,)), ((), ())), preferred_element_type=jnp.float32
    )


def product_over_rows(left, right):
    return lax.dot_general(
        left, right, (((0,), (0,)), ((), ())), preferred_element_type=jnp.float32
    )


def depthwise(signal, edge_rows, weights):
    tap_count = weights.shape[0]
    span_len = signal.shape[1]
    padded = jnp.concatenate([edge_rows, signal], axis=1).astype(jnp.float32)
    wide_taps = weights.astype(jnp.float32)
    total = wide_taps[0] * padded[:, 0:span_len]
    for offset in range(1, tap_count):
        total = total + wide_taps[offset] * padded[:, offset : offset + span_len]
    return (total, padded)


def depthwise_back(grad_conv, edge_rows, weights, padded):
    tap_count = weights.shape[0]
    span_len = grad_conv.shape[1]
    wide_taps = weights.astype(jnp.float32)
    extended = jnp.concatenate([grad_conv, edge_rows], axis=1)
    grad_signal = wide_taps[tap_count - 1] * extended[:, 0:span_len]
    for offset in range(1, tap_count):
        grad_signal = (
            grad_signal
            + wide_taps[tap_count - 1 - offset] * extended[:, offset : offset + span_len]
        )
    grad_taps = jnp.stack(
        [
            jnp.sum(grad_conv * padded[:, offset : offset + span_len], axis=(0, 1))
            for offset in range(tap_count)
        ]
    )
    return (grad_signal, grad_taps)


def silu_slope(value):
    sigma = jax.nn.sigmoid(value)
    return sigma * (1.0 + value * (1.0 - sigma))


MESH = pl.DeviceIdType.MESH
IN_VMEM = pl.BlockSpec(memory_space=pltpu.VMEM)


def group_place():
    places = lax.axis_size("context")
    count = lax.axis_size("shards") * places
    mine = lax.axis_index("shards") * places + lax.axis_index("context")
    return count, mine


def group_peer(steps):
    count, mine = group_place()
    peer = lax.rem(mine + steps, count)
    places = lax.axis_size("context")
    return peer, {"shards": peer // places, "context": lax.rem(peer, places)}


def meet(devices):
    barrier = pltpu.get_barrier_semaphore()
    for device in devices:
        pl.semaphore_signal(barrier, inc=1, device_id=device, device_id_type=MESH)
    pl.semaphore_wait(barrier, len(devices))


def remote(source, target, sent, landed, device):
    return pltpu.make_async_remote_copy(
        src_ref=source,
        dst_ref=target,
        send_sem=sent,
        recv_sem=landed,
        device_id=device,
        device_id_type=MESH,
    )


def tensor_places():
    mine = lax.axis_index("tensor")
    return mine, mine + 1 - 2 * lax.rem(mine, 2), lax.rem(mine + 2, 4)


def scatter_kernel(
    rows, weights, own, weights_own, from_mate, from_partner, outgoing, arrived, t_sent, t_landed,
    w_sent, w_landed
):
    count, place = group_place()
    mine, mate, partner = tensor_places()
    beyond = lax.rem(mate + 2, 4)
    meet(
        [{"tensor": mate}, {"tensor": partner}]
        + [group_peer(step)[1] for step in range(1, count)]
    )
    first = remote(
        rows.at[beyond], from_mate.at[0], t_sent.at[0], t_landed.at[0], {"tensor": mate}
    )
    second = remote(rows.at[mate], from_mate.at[1], t_sent.at[1], t_landed.at[1], {"tensor": mate})
    first.start()
    second.start()
    copies = []
    for step in range(1, count):
        peer, device = group_peer(step)
        copies.append(
            remote(
                weights.at[peer],
                arrived.at[step - 1],
                w_sent.at[step - 1],
                w_landed.at[step - 1],
                device,
            )
        )
        copies[-1].start()
    first.wait()
    outgoing[...] = (
        rows[partner].astype(jnp.float32) + from_mate[0].astype(jnp.float32)
    ).astype(jnp.bfloat16)
    across = remote(outgoing, from_partner, t_sent.at[2], t_landed.at[2], {"tensor": partner})
    across.start()
    second.wait()
    own[...] = rows[mine].astype(jnp.float32) + from_mate[1].astype(jnp.float32)
    across.wait()
    own[...] = own[...] + from_partner[...].astype(jnp.float32)
    weights_own[...] = weights[place].astype(jnp.float32)
    for step in range(1, count):
        copies[step - 1].wait()
        weights_own[...] = weights_own[...] + arrived[step - 1].astype(jnp.float32)


def scatter_sums(rows, weights):
    _, length, width = rows.shape
    count, chunk, columns = weights.shape
    return pl.pallas_call(
        scatter_kernel,
        out_shape=(
            jax.ShapeDtypeStruct((length, width), jnp.float32),
            jax.ShapeDtypeStruct((chunk, columns), jnp.float32),
        ),
        in_specs=[IN_VMEM, IN_VMEM],
        out_specs=(IN_VMEM, IN_VMEM),
        scratch_shapes=[
            pltpu.VMEM((2, length, width), jnp.bfloat16),
            pltpu.VMEM((length, width), jnp.bfloat16),
            pltpu.VMEM((length, width), jnp.bfloat16),
            pltpu.VMEM((count - 1, chunk, columns), jnp.bfloat16),
            pltpu.SemaphoreType.DMA((3,)),
            pltpu.SemaphoreType.DMA((3,)),
            pltpu.SemaphoreType.DMA((count - 1,)),
            pltpu.SemaphoreType.DMA((count - 1,)),
        ],
        compiler_params=pltpu.CompilerParams(
            collective_id=1, has_side_effects=True, vmem_limit_bytes=40 * 2**20
        ),
    )(rows, weights)


def gather_kernel(
    own, weights, small, full, weights_sum, small_sum, w_arrived, s_arrived, w_part, s_part,
    w_tensor, s_tensor, t_sent, t_landed, g_sent, g_landed, h_sent, h_landed
):
    count, place = group_place()
    mine, mate, partner = tensor_places()
    others = [{"tensor": lax.rem(mine + step, 4)} for step in range(1, 4)]
    meet(others + [group_peer(step)[1] for step in range(1, count)])
    across = remote(own, full.at[mine], t_sent.at[0], t_landed.at[0], {"tensor": partner})
    aside = remote(own, full.at[mine], t_sent.at[1], t_landed.at[1], {"tensor": mate})
    across.start()
    aside.start()
    copies = []
    for step in range(1, count):
        peer, device = group_peer(step)
        at = step - 1
        pair = (
            remote(small, s_arrived.at[at], g_sent.at[0, at], g_landed.at[0, at], device),
            remote(
                weights.at[peer], w_arrived.at[at], g_sent.at[1, at], g_landed.at[1, at], device
            ),
        )
        pair[0].start()
        pair[1].start()
        copies.append(pair)
    full[pl.ds(mine, 1)] = own[...][None]
    s_part[...] = small[...]
    w_part[...] = weights[place].astype(jnp.float32)
    for step in range(1, count):
        for copy in copies[step - 1]:
            copy.wait()
        s_part[...] = s_part[...] + s_arrived[step - 1]
        w_part[...] = w_part[...] + w_arrived[step - 1].astype(jnp.float32)
    last = []
    for at, device in enumerate(others):
        last.append(
            (
                remote(s_part, s_tensor.at[at], h_sent.at[0, at], h_landed.at[0, at], device),
                remote(w_part, w_tensor.at[at], h_sent.at[1, at], h_landed.at[1, at], device),
            )
        )
        last[-1][0].start()
        last[-1][1].start()
    across.wait()
    onward = remote(
        full.at[partner], full.at[partner], t_sent.at[2], t_landed.at[2], {"tensor": mate}
    )
    onward.start()
    for pair in last:
        for copy in pair:
            copy.wait()
    whole = small.shape[0] // 2
    small_sum[...] = s_part[...]
    small_sum[pl.ds(0, whole)] = (
        s_part[pl.ds(0, whole)]
        + s_tensor[0, pl.ds(0, whole)]
        + s_tensor[1, pl.ds(0, whole)]
        + s_tensor[2, pl.ds(0, whole)]
    )
    weights_sum[...] = w_part[...] + w_tensor[0] + w_tensor[1] + w_tensor[2]
    aside.wait()
    onward.wait()


def gather_sums(own, weights, small):
    length, width = own.shape
    count, chunk, columns = weights.shape
    return pl.pallas_call(
        gather_kernel,
        out_shape=(
            jax.ShapeDtypeStruct((4, length, width), jnp.bfloat16),
            jax.ShapeDtypeStruct((chunk, columns), jnp.float32),
            jax.ShapeDtypeStruct(small.shape, jnp.float32),
        ),
        in_specs=[IN_VMEM, IN_VMEM, IN_VMEM],
        out_specs=(IN_VMEM, IN_VMEM, IN_VMEM),
        scratch_shapes=[
            pltpu.VMEM((count - 1, chunk, columns), jnp.bfloat16),
            pltpu.VMEM((count - 1,) + small.shape, jnp.float32),
            pltpu.VMEM((chunk, columns), jnp.float32),
            pltpu.VMEM(small.shape, jnp.float32),
            pltpu.VMEM((3, chunk, columns), jnp.float32),
            pltpu.VMEM((3,) + small.shape, jnp.float32),
            pltpu.SemaphoreType.DMA((3,)),
            pltpu.SemaphoreType.DMA((3,)),
            pltpu.SemaphoreType.DMA((2, count - 1)),
            pltpu.SemaphoreType.DMA((2, count - 1)),
            pltpu.SemaphoreType.DMA((2, 3)),
            pltpu.SemaphoreType.DMA((2, 3)),
        ],
        compiler_params=pltpu.CompilerParams(
            collective_id=2, has_side_effects=True, vmem_limit_bytes=40 * 2**20
        ),
    )(own, weights, small)


def on_device(
    tokens,
    norm_gain,
    w_z,
    w_x,
    w_bc,
    w_dt,
    conv_x,
    conv_bc,
    dt_bias,
    a_log,
    skip,
    gate_gain,
    w_out,
    cotangent,
):
    seq_count, span_len, model_width = tokens.shape
    row_count = seq_count * span_len
    head_count = dt_bias.shape[0]
    state_size = w_bc.shape[1] // 2
    tap_count = conv_x.shape[0]
    block_count = span_len // BLOCK
    inner_part = w_z.shape[1]
    packed = jnp.concatenate(
        [w_x, w_bc, jnp.pad(w_dt, ((0, 0), (0, 128 - head_count)))], axis=1
    )
    full = lax.all_gather(packed, "shards", axis=0, tiled=True)
    later = lax.all_gather(
        jnp.concatenate([w_z, w_out.T], axis=1), "shards", axis=0, tiled=True
    )
    full_x = full[:, :inner_part]
    full_bc = full[:, inner_part : inner_part + 2 * state_size]
    full_dt = full[:, inner_part + 2 * state_size : inner_part + 2 * state_size + head_count]
    full_z = later[:, :inner_part]
    out_t = later[:, inner_part:]
    inner_width = full_z.shape[1]
    head_width = inner_width // head_count
    flat_rows = tokens.reshape(row_count, model_width).astype(jnp.float32)
    row_scale = lax.rsqrt(jnp.mean(flat_rows * flat_rows, axis=1, keepdims=True) + epsilon)
    unit_rows = flat_rows * row_scale
    gain_input = norm_gain.astype(jnp.float32)
    normed = (unit_rows * gain_input).astype(jnp.bfloat16)
    fronts = product(normed, full)
    gate_value = product(normed, full_z)
    pre = fronts[:, : inner_part + 2 * state_size].astype(jnp.bfloat16)
    pre = pre.reshape(seq_count, span_len, inner_part + 2 * state_size)
    x_pre, bc_pre = pre[..., :inner_part], pre[..., inner_part:]
    dt_raw = fronts[:, inner_part + 2 * state_size : inner_part + 2 * state_size + head_count]
    edge = from_behind(pre[:, span_len - tap_count + 1 :], "context", 1)
    x_edge, bc_edge = edge[..., :inner_part], edge[..., inner_part:]
    x_conv, x_padded = depthwise(x_pre, x_edge, conv_x)
    bc_conv, bc_padded = depthwise(bc_pre, bc_edge, conv_bc)
    x_act = jax.nn.silu(x_conv).astype(jnp.bfloat16)
    bc_act = jax.nn.silu(bc_conv).astype(jnp.bfloat16)
    x_blocks = x_act.reshape(seq_count, block_count, BLOCK, head_count, head_width)
    b_in = bc_act[:, :, :state_size].reshape(seq_count, block_count, BLOCK, state_size)
    c_in = bc_act[:, :, state_size:].reshape(seq_count, block_count, BLOCK, state_size)
    pre_step = dt_raw + dt_bias
    step_size = jax.nn.softplus(pre_step)
    rate = -jnp.exp(a_log)
    step_heads = jnp.transpose(
        step_size.reshape(seq_count, block_count, BLOCK, head_count), (0, 1, 3, 2)
    )
    lower = jnp.tril(jnp.ones((BLOCK, BLOCK), jnp.float32))
    decay_sum = jnp.einsum("schj,ij->schi", step_heads * rate[:, None], lower, precision=highest)
    last_sum = decay_sum[..., -1]
    causal = lax.broadcasted_iota(jnp.int32, (BLOCK, BLOCK), 0) >= lax.broadcasted_iota(
        jnp.int32, (BLOCK, BLOCK), 1
    )
    gram_matrix = jnp.einsum("scin,scjn->scij", c_in, b_in, preferred_element_type=jnp.float32)
    spacing = decay_sum[..., :, None] - decay_sum[..., None, :]
    within = jnp.where(causal, jnp.exp(jnp.where(causal, spacing, 0.0)), 0.0)
    masked_within = within * step_heads[..., None, :]
    mix_full = gram_matrix[:, :, None] * masked_within
    mixing = mix_full.astype(jnp.bfloat16)
    intra = jnp.einsum("schij,scjhp->scihp", mixing, x_blocks, preferred_element_type=jnp.float32)
    toward = jnp.exp(last_sum[..., None] - decay_sum) * step_heads
    b_wide = b_in.astype(jnp.float32)
    loaded = (b_wide[:, :, None] * toward[..., None]).astype(jnp.bfloat16)
    fresh_state = jnp.einsum(
        "schjn,scjhp->schnp", loaded, x_blocks, preferred_element_type=jnp.float32
    )
    carried = jnp.zeros((seq_count, head_count, state_size, head_width), jnp.float32)
    entering = []
    for index in range(block_count):
        entering.append(carried)
        carried = jnp.exp(last_sum[:, index])[:, :, None, None] * carried + fresh_state[:, index]
    device_total = jnp.sum(last_sum, axis=1)
    device_decay = jnp.exp(device_total)
    incoming = from_behind(carried.astype(jnp.bfloat16), "context", 1).astype(jnp.float32)
    after_sum = jnp.cumsum(last_sum, axis=1)
    start_decay = jnp.exp(after_sum - last_sum)
    enter_true = jnp.stack(entering, axis=1) + start_decay[..., None, None] * incoming[:, None]
    enter_low = enter_true.astype(jnp.bfloat16)
    reached = jnp.einsum("scin,schnp->scihp", c_in, enter_low, preferred_element_type=jnp.float32)
    growth = jnp.exp(jnp.transpose(decay_sum, (0, 1, 3, 2)))
    x_wide = x_blocks.astype(jnp.float32)
    scanned = intra + growth[..., None] * reached + skip[:, None] * x_wide
    scanned = scanned.reshape(row_count, inner_width)
    sigma_gate = jax.nn.sigmoid(gate_value)
    silu_gate = gate_value * sigma_gate
    gated_out = scanned * silu_gate
    gain_gate = gate_gain.astype(jnp.float32)
    weighted = (gated_out * gain_gate).astype(jnp.bfloat16)
    partial_value = product_transposed(weighted, out_t)
    square_sums = jnp.sum(gated_out * gated_out, axis=1)
    grad_rows = cotangent.reshape(row_count, model_width).astype(jnp.float32)
    scale_part = jnp.sum(grad_rows * partial_value, axis=1)
    squares, grad_scale = lax.psum(jnp.stack([square_sums, scale_part]), "tensor")
    own_rows = row_count // lax.axis_size("tensor")
    own_at = lax.axis_index("tensor") * own_rows

    def own(value):
        return lax.dynamic_slice_in_dim(value, own_at, own_rows, 0)

    out_scale = lax.rsqrt(squares / INNER + epsilon)
    own_projected = lax.psum_scatter(
        partial_value.astype(jnp.bfloat16), "tensor", scatter_dimension=0, tiled=True
    ).astype(jnp.float32)
    own_mixed = (own(flat_rows) + own_projected * own(out_scale)[:, None]).astype(jnp.bfloat16)
    mixed = lax.all_gather(own_mixed, "tensor", axis=0, tiled=True).reshape(tokens.shape)
    grad_spread = -0.5 * grad_scale * out_scale * out_scale * out_scale
    grad_proj = (grad_rows * out_scale[:, None]).astype(jnp.bfloat16)
    grad_weighted = product(grad_proj, out_t)
    grad_out_t = product_over_rows(grad_proj, weighted)
    grad_gate_gain = jnp.sum(grad_weighted * gated_out, axis=0)
    grad_gated = grad_weighted * gain_gate + 2.0 / INNER * grad_spread[:, None] * gated_out
    grad_scanned = (grad_gated * silu_gate).astype(jnp.bfloat16)
    grad_gate = (
        grad_gated * scanned * sigma_gate * (1.0 + gate_value * (1.0 - sigma_gate))
    ).astype(jnp.bfloat16)
    grad_w_z = product_over_rows(normed, grad_gate)
    grad_blocks = grad_scanned.reshape(seq_count, block_count, BLOCK, head_count, head_width)
    grad_wide = grad_blocks.astype(jnp.float32)
    grad_skip = jnp.sum(grad_wide * x_wide, axis=(0, 1, 2, 4))
    grad_reached = grad_wide * growth[..., None]
    reached_low = grad_reached.astype(jnp.bfloat16)
    from_output = jnp.einsum("scin,scihp->schnp", c_in, reached_low, preferred_element_type=jnp.float32)
    carried_back = jnp.zeros_like(carried)
    leaving = []
    for index in range(block_count - 1, -1, -1):
        leaving.append(carried_back)
        carried_back = (
            from_output[:, index] + jnp.exp(last_sum[:, index])[:, :, None, None] * carried_back
        )
    outgoing = from_behind(carried_back.astype(jnp.bfloat16), "context", -1).astype(jnp.float32)
    end_decay = jnp.exp(device_total[:, None] - after_sum)
    leave_true = jnp.stack(leaving[::-1], axis=1) + end_decay[..., None, None] * outgoing[:, None]
    leave_low = leave_true.astype(jnp.bfloat16)
    grad_x_blocks = skip[:, None] * grad_wide
    grad_x_blocks = grad_x_blocks + jnp.einsum(
        "schij,scihp->scjhp", mixing, grad_blocks, preferred_element_type=jnp.float32
    )
    grad_x_blocks = grad_x_blocks + jnp.einsum(
        "schjn,schnp->scjhp", loaded, leave_low, preferred_element_type=jnp.float32
    )
    grad_mix = jnp.einsum(
        "scihp,scjhp->schij", grad_blocks, x_blocks, preferred_element_type=jnp.float32
    )
    grad_gram = jnp.sum(grad_mix * masked_within, axis=2).astype(jnp.bfloat16)
    grad_step = jnp.sum(grad_mix * gram_matrix[:, :, None] * within, axis=3)
    spread_term = grad_mix * mix_full
    grad_cum = jnp.sum(spread_term, axis=4) - jnp.sum(spread_term, axis=3)
    grad_c_in = jnp.einsum("scij,scjn->scin", grad_gram, b_in, preferred_element_type=jnp.float32)
    grad_c_in = grad_c_in + jnp.einsum(
        "scihp,schnp->scin", reached_low, enter_low, preferred_element_type=jnp.float32
    )
    grad_b_in = jnp.einsum("scij,scin->scjn", grad_gram, c_in, preferred_element_type=jnp.float32)
    grad_cum = grad_cum + jnp.transpose(jnp.sum(grad_reached * reached, axis=4), (0, 1, 3, 2))
    grad_last = jnp.sum(leave_true * enter_true, axis=(3, 4)) * jnp.exp(last_sum)
    grad_loaded = jnp.einsum("scjhp,schnp->schjn", x_blocks, leave_low, preferred_element_type=jnp.float32)
    grad_b_in = grad_b_in + jnp.sum(grad_loaded * toward[..., None], axis=2)
    touch = jnp.sum(grad_loaded * b_wide[:, :, None], axis=4)
    touch_part = touch * toward
    grad_step = grad_step + touch * jnp.exp(last_sum[..., None] - decay_sum)
    grad_last = grad_last + jnp.sum(touch_part, axis=3)
    grad_cum = (grad_cum - touch_part).at[..., -1].add(grad_last)
    grad_log = jnp.einsum("schi,ij->schj", grad_cum, lower, precision=highest)
    grad_step = grad_step + grad_log * rate[:, None]
    grad_a_log = jnp.sum(grad_log * step_heads, axis=(0, 1, 3)) * rate
    grad_pre = jnp.transpose(grad_step, (0, 1, 3, 2)).reshape(
        row_count, head_count
    ) * jax.nn.sigmoid(pre_step)
    grad_dt_bias = jnp.sum(grad_pre, axis=0)
    grad_dt_raw = grad_pre.astype(jnp.bfloat16)
    grad_x_conv = grad_x_blocks.reshape(seq_count, span_len, inner_width) * silu_slope(x_conv)
    grad_bc_act = jnp.concatenate([grad_b_in, grad_c_in], axis=3).reshape(
        seq_count, span_len, 2 * state_size
    )
    grad_bc_conv = grad_bc_act * silu_slope(bc_conv)
    following = from_behind(
        jnp.concatenate(
            [grad_x_conv[:, : tap_count - 1], grad_bc_conv[:, : tap_count - 1]], axis=2
        ),
        "context",
        -1,
    )
    x_next, bc_next = following[..., :inner_width], following[..., inner_width:]
    grad_x_signal, grad_conv_x = depthwise_back(grad_x_conv, x_next, conv_x, x_padded)
    grad_bc_signal, conv_bc_part = depthwise_back(grad_bc_conv, bc_next, conv_bc, bc_padded)
    grad_x_pre = grad_x_signal.reshape(row_count, inner_width).astype(jnp.bfloat16)
    normed_part = (
        product_transposed(grad_gate, full_z)
        + product_transposed(grad_x_pre, full_x)
        + product_transposed(grad_dt_raw, full_dt)
    )
    group_count = group_place()[0]
    grad_w_x = product_over_rows(normed, grad_x_pre)
    grad_w_dt = product_over_rows(normed, grad_dt_raw)
    rows_all = jnp.concatenate(
        [normed_part, grad_bc_signal.reshape(row_count, 2 * state_size)], axis=1
    ).astype(jnp.bfloat16)
    grads_all = jnp.concatenate(
        [grad_w_x, grad_w_z, grad_out_t, jnp.pad(grad_w_dt, ((0, 0), (0, 128 - head_count)))],
        axis=1,
    ).astype(jnp.bfloat16)
    own_sums, final_all = scatter_sums(
        rows_all.reshape(4, own_rows, -1), grads_all.reshape(group_count, -1, grads_all.shape[1])
    )
    own_grad = own_sums[:, :model_width]
    own_bc = own_sums[:, model_width:].astype(jnp.bfloat16)
    final_x = final_all[:, :inner_width]
    final_z = final_all[:, inner_width : 2 * inner_width]
    final_out = final_all[:, 2 * inner_width : 3 * inner_width].T
    final_dt = final_all[:, 3 * inner_width : 3 * inner_width + head_count]
    own_grad = own_grad + product_transposed(own_bc, full_bc)
    own_unit = own(unit_rows)
    grad_norm_gain = jnp.sum(own_grad * own_unit, axis=0)
    grad_unit = own_grad * gain_input
    own_tokens = own(grad_rows) + own(row_scale) * (
        grad_unit - own_unit * jnp.mean(grad_unit * own_unit, axis=1, keepdims=True)
    )
    grad_w_bc = product_over_rows(own(normed), own_bc).astype(jnp.bfloat16)
    whole = jnp.concatenate([grad_norm_gain, conv_bc_part.reshape(-1)])
    by_tensor = jnp.concatenate(
        [grad_conv_x.reshape(-1), grad_gate_gain, grad_dt_bias, grad_a_log, grad_skip]
    )
    half = -(-max(whole.shape[0], by_tensor.shape[0]) // 1024) * 1024
    small = jnp.concatenate(
        [
            jnp.pad(whole, (0, half - whole.shape[0])),
            jnp.pad(by_tensor, (0, half - by_tensor.shape[0])),
        ]
    ).reshape(-1, 128)
    gathered, final_bc, sums = gather_sums(
        own_tokens.astype(jnp.bfloat16), grad_w_bc.reshape(group_count, -1, 2 * state_size), small
    )
    grad_tokens = gathered.astype(jnp.float32)
    sums = sums.reshape(2, half)
    norm_sum = sums[0, :model_width]
    conv_bc_sum = sums[0, model_width : whole.shape[0]].reshape(conv_bc.shape)
    mine = sums[1, : by_tensor.shape[0]]
    at = tap_count * inner_width
    conv_x_sum = mine[:at].reshape(tap_count, inner_width)
    gate_gain_sum = mine[at : at + inner_width]
    heads_sum = mine[at + inner_width :].reshape(3, head_count)
    return (
        mixed,
        grad_tokens.reshape(seq_count, span_len, model_width),
        norm_sum,
        final_z,
        final_x,
        final_bc,
        final_dt,
        conv_x_sum,
        conv_bc_sum,
        heads_sum[0],
        heads_sum[1],
        heads_sum[2],
        gate_gain_sum,
        final_out,
    )


def solution(mesh):
    placed = (
        P("shards", "context", None),
        P(),
        P("shards", "tensor"),
        P("shards", "tensor"),
        P("shards", None),
        P("shards", "tensor"),
        P(None, "tensor"),
        P(),
        P("tensor"),
        P("tensor"),
        P("tensor"),
        P("tensor"),
        P("tensor", "shards"),
        P("shards", "context", None),
    )
    return jax.shard_map(
        on_device,
        mesh=mesh,
        in_specs=placed,
        out_specs=(
            P("shards", "context", None),
            P("shards", "context", None),
            P(),
            P(("shards", "context"), "tensor"),
            P(("shards", "context"), "tensor"),
            P(("shards", "context"), None),
            P(("shards", "context"), "tensor"),
            P(None, "tensor"),
            P(),
            P("tensor"),
            P("tensor"),
            P("tensor"),
            P("tensor"),
            P("tensor", ("shards", "context")),
        ),
        check_vma=False,
    )
```
